256 devices in a mesh: dp: 4 (over x_hi, core), mp: 64 (over x_lo, y, z).
Axes of the slice: x: 4 (x_hi: 2, x_lo: 2; x = x_hi * 2 + x_lo), y: 4, z: 8, core: 2. Of those that a mesh axis runs over, the one named last changes fastest.
Arguments:
- tokens: bfloat16 [2304, 4096], P(('dp', 'mp')), may hold values from -6 to 6
- out_grad: bfloat16 [2304, 4096], P(('dp', 'mp')), may hold values from -6 to 6
- gate_weight: bfloat16 [16384, 4096], P('mp', 'dp'), may hold values from -0.125 to 0.125
- up_weight: bfloat16 [16384, 4096], P('mp', 'dp'), may hold values from -0.125 to 0.125
- down_weight: bfloat16 [16384, 4096], P('mp', 'dp'), may hold values from -0.0625 to 0.0625
- block_mask: int32 [3, 128, 32], replicated, may hold values 0 or 1
- assignment: int32 [128], P('mp'), may hold values from 0 to 127, each once
Outputs:
- input_grad: bfloat16 [2304, 4096], P(('dp', 'mp'))
- gate_grad_out: bfloat16 [16384, 4096], P('mp', 'dp')
- up_grad_out: bfloat16 [16384, 4096], P('mp', 'dp')
- down_grad_out: bfloat16 [16384, 4096], P('mp', 'dp')
The draws below stay inside these ranges and needn't reach their ends.
Inputs may be any that keep to these rules, and one draw needn't show every extreme that they name: `assignment`: each of the 128 panel numbers appears once.
All inputs are finite; a program needn't handle non-finite values.
Results may differ from the reference program's by a relative error of at most 0.0049.
Values may be sent and summed in bfloat16 or wider, within the bound.
No kernel may reach another device: no remote copies, remote signals or barrier semaphores. Data moves between devices by JAX's collectives and lax.ppermute only.
A program may use at most 128 MiB of HBM per device.

```python
import jax
import jax.numpy as jnp

D = 4096
BLK = 128
FF = 16384
PANELS = 128
DB = 32
TOKENS = 2304


def set_ends(result, stream_key, smallest, top_value):
    longest = result.shape.index(max(result.shape))
    spots = []
    for shift in (0, 1):
        where = [jax.random.randint(jax.random.fold_in(stream_key, axis), (), 0, length) for axis, length in enumerate(result.shape)]
        where[longest] = (where[longest] + shift) % result.shape[longest]
        spots.append(tuple(where))
    return result.at[spots[0]].set(smallest).at[spots[1]].set(top_value)


def levels(key, shape, shards, smallest, largest):
    level = 1.0
    for position, blocks in shards:
        draws = jax.random.uniform(jax.random.fold_in(jax.random.fold_in(key, 6), position), (blocks,), jnp.float32, smallest / len(shards), largest / len(shards))
        level = level * jnp.repeat(jnp.exp(draws), shape[position] // blocks).reshape((-1,) + (1,) * (len(shape) - 1 - position))
    return level


def gaussian(stream_key, shape, scale, reach, cuts=(), kind=jnp.bfloat16):
    entries = jax.random.normal(stream_key, shape, jnp.float32) * scale
    if len(cuts) > 0:
        entries = levels(stream_key, shape, cuts, -0.22, 0.18) * entries
    return jnp.clip(entries, min=-reach, max=reach).astype(kind)


def setup_inputs(seed: int = 0) -> dict:
    seeds = jax.random.split(jax.random.key(seed), 8)
    tokens = gaussian(seeds[0], (TOKENS, D), 1.0, 6.0, ((0, 256),))
    out_grad = gaussian(seeds[1], (TOKENS, D), 1.0, 6.0, ((0, 256),))
    gate_weight = gaussian(seeds[2], (FF, D), (D // 2) ** -0.5, 0.125, ((0, 64), (1, 4)))
    up_weight = gaussian(seeds[3], (FF, D), (D // 2) ** -0.5, 0.125, ((0, 64), (1, 4)))
    down_weight = gaussian(seeds[4], (FF, D), (FF // 2) ** -0.5, 0.0625, ((0, 64), (1, 4)))
    block_mask = set_ends((jax.random.randint(seeds[5], (3, PANELS, DB), 0, 2) < 1).astype(jnp.int32), jax.random.fold_in(seeds[5], 1), 0, 1)
    assignment = jax.random.permutation(seeds[6], PANELS).astype(jnp.int32)
    return {"tokens": tokens, "out_grad": out_grad, "gate_weight": gate_weight, "up_weight": up_weight, "down_weight": down_weight, "block_mask": block_mask, "assignment": assignment}


def spread_mask(rows):
    wide = jnp.repeat(jnp.repeat(rows, BLK, axis=0), BLK, axis=1)
    return wide.astype(jnp.bfloat16)


def reference(tokens, out_grad, gate_weight, up_weight, down_weight, block_mask, assignment):
    slot_mask = block_mask[:, assignment, :]
    gate_keep = spread_mask(slot_mask[0])
    up_keep = spread_mask(slot_mask[1])
    down_keep = spread_mask(slot_mask[2])
    gate_m = gate_weight * gate_keep
    up_m = up_weight * up_keep
    down_m = down_weight * down_keep
    gate_pre = jnp.dot(tokens, gate_m.T, preferred_element_type=jnp.float32)
    up_pre = jnp.dot(tokens, up_m.T, preferred_element_type=jnp.float32)
    sigma = jax.nn.sigmoid(gate_pre)
    swish = gate_pre * sigma
    hidden = (swish * up_pre).astype(jnp.bfloat16)
    hidden_grad = jnp.dot(out_grad, down_m.T, preferred_element_type=jnp.float32)
    up_grad = (hidden_grad * swish).astype(jnp.bfloat16)
    gate_grad = (hidden_grad * up_pre * sigma * (1.0 + gate_pre * (1.0 - sigma))).astype(jnp.bfloat16)
    input_grad = jnp.dot(gate_grad, gate_m, preferred_element_type=jnp.float32)
    input_grad = input_grad + jnp.dot(up_grad, up_m, preferred_element_type=jnp.float32)
    gate_out = jnp.dot(gate_grad.T, tokens, preferred_element_type=jnp.float32) * gate_keep
    up_out = jnp.dot(up_grad.T, tokens, preferred_element_type=jnp.float32) * up_keep
    down_out = jnp.dot(hidden.T, out_grad, preferred_element_type=jnp.float32) * down_keep
    return (input_grad.astype(jnp.bfloat16), gate_out.astype(jnp.bfloat16),
            up_out.astype(jnp.bfloat16), down_out.astype(jnp.bfloat16))
```

```python
import jax
import jax.numpy as jnp
from jax import lax
from jax.sharding import Mesh
from jax.sharding import PartitionSpec as P

BLK = 128
AXES = ("x_hi", "core", "x_lo", "y", "z")
SIZES = (2, 2, 2, 4, 8)
DP = ("x_hi", "core")
MP = ("x_lo", "y", "z")
BF = jnp.bfloat16
F32 = jnp.float32


def fetch(block, axis, offset):
    size = SIZES[AXES.index(axis)]
    return lax.ppermute(block, axis, [(i, (i - offset) % size) for i in range(size)])


def ring_gather(block, axis):
    size = SIZES[AXES.index(axis)]
    half = size // 2
    found = {0: block}
    for step in range(1, half):
        found[step] = fetch(found[step - 1], axis, 1)
        found[-step % size] = fetch(found[(1 - step) % size], axis, -1)
    cut = block.shape[1] // 2
    found[half] = jnp.concatenate(
        [fetch(found[half - 1][:, :cut], axis, 1), fetch(found[half + 1][:, cut:], axis, -1)], axis=1
    )
    return [found[offset] for offset in range(size)]


def ring_scatter(parts, axis):
    size = SIZES[AXES.index(axis)]
    half = size // 2
    cut = parts[0].shape[1] // 2
    up = parts[half][:, :cut].astype(BF)
    down = parts[half][:, cut:].astype(BF)
    up = fetch(up, axis, -1).astype(F32)
    down = fetch(down, axis, 1).astype(F32)
    up = jnp.concatenate([parts[half - 1][:, :cut] + up, parts[half - 1][:, cut:]], axis=1)
    down = jnp.concatenate([parts[half + 1][:, :cut], parts[half + 1][:, cut:] + down], axis=1)
    for step in range(half - 2, -1, -1):
        up = fetch(up.astype(BF), axis, -1).astype(F32)
        down = fetch(down.astype(BF), axis, 1).astype(F32)
        if step > 0:
            up = parts[step] + up
            down = parts[-step % size] + down
    return parts[0] + up + down


def spread_mask(rows):
    return jnp.repeat(jnp.repeat(rows, BLK, axis=1), BLK, axis=2).astype(BF)


def kept_masks(block_mask, assignment, col_blocks):
    first_block = lax.axis_index(DP) * col_blocks
    panel_ids = lax.broadcasted_iota(jnp.int32, (assignment.shape[0], block_mask.shape[1]), 1)
    selector = (assignment[:, None] == panel_ids).astype(F32)
    slot_mask = jnp.einsum("sp,mpb->msb", selector, block_mask.astype(F32))
    return spread_mask(lax.dynamic_slice_in_dim(slot_mask, first_block, col_blocks, 2))


def gather_weights(kept):
    x_hi, core = lax.axis_index("x_hi"), lax.axis_index("core")
    other = fetch(kept, "x_hi", 1)
    mine = jnp.where(x_hi == 0, jnp.stack([kept, other]), jnp.stack([other, kept]))
    theirs = fetch(mine, "core", 1)
    both = jnp.where(core == 0, jnp.stack([mine, theirs], 1), jnp.stack([theirs, mine], 1))
    return jnp.concatenate([both[0, 0], both[0, 1], both[1, 0], both[1, 1]], axis=-1)


def scatter_weight_grads(parts):
    x_hi, core = lax.axis_index("x_hi"), lax.axis_index("core")
    cols = parts.shape[-1] // 4
    blocks = [parts[..., i * cols : (i + 1) * cols] for i in range(4)]
    give = jnp.stack([jnp.where(core == 0, blocks[2 * i + 1], blocks[2 * i]) for i in range(2)])
    keep = jnp.stack([jnp.where(core == 0, blocks[2 * i], blocks[2 * i + 1]) for i in range(2)])
    both = keep + fetch(give.astype(BF), "core", 1).astype(F32)
    far = jnp.where(x_hi == 0, both[1], both[0]).astype(BF)
    near = jnp.where(x_hi == 0, both[0], both[1])
    return near + fetch(far, "x_hi", 1).astype(F32)


def per_device(tokens, out_grad, gate_weight, up_weight, down_weight, block_mask, assignment):
    own, width = tokens.shape
    hid = gate_weight.shape[0]
    keep = kept_masks(block_mask, assignment, gate_weight.shape[1] // BLK)
    full = gather_weights(jnp.stack([gate_weight, up_weight, down_weight]) * keep)
    gate_up = full[:2].reshape(2 * hid, width)
    down = full[2]

    pair = jnp.concatenate([tokens, out_grad], axis=0)
    other = fetch(pair, "x_lo", 1)
    tok = jnp.concatenate([tokens, other[:own]], axis=0)
    grd = jnp.concatenate([out_grad, other[own:]], axis=0)
    tok = jnp.concatenate(ring_gather(tok, "y"), axis=0)
    grd = jnp.concatenate(ring_gather(grd, "z"), axis=0)
    tok = jnp.concatenate(ring_gather(tok, "z"), axis=0)
    grd = jnp.concatenate(ring_gather(grd, "y"), axis=0)

    n_y, n_z, unit = SIZES[3], SIZES[4], 2 * own

    def to_y_first(rows):
        return rows.reshape(n_z, n_y, unit, -1).transpose(1, 0, 2, 3).reshape(rows.shape)

    def to_z_first(rows):
        return rows.reshape(n_y, n_z, unit, -1).transpose(1, 0, 2, 3).reshape(rows.shape)

    pre = jnp.einsum("td,hd->th", tok, gate_up, preferred_element_type=F32)
    gate_pre, up_pre = pre[:, :hid], pre[:, hid:]
    hidden_grad = to_z_first(jnp.einsum("td,hd->th", grd, down, preferred_element_type=F32))
    sigma = jax.nn.sigmoid(gate_pre)
    swish = gate_pre * sigma
    hidden = to_y_first((swish * up_pre).astype(BF))
    up_grad = (hidden_grad * swish).astype(BF)
    gate_grad = (hidden_grad * up_pre * sigma * (1.0 + gate_pre * (1.0 - sigma))).astype(BF)
    both_grads = jnp.concatenate([gate_grad, up_grad], axis=1)

    cut = width // 2
    left = jnp.dot(both_grads, gate_up[:, :cut], preferred_element_type=F32)
    right = jnp.dot(to_y_first(both_grads), gate_up[:, cut:], preferred_element_type=F32)
    left = ring_scatter(jnp.split(left, n_z), "z")
    right = ring_scatter(jnp.split(right, n_y), "y")
    left = ring_scatter(jnp.split(left, n_y), "y")
    right = ring_scatter(jnp.split(right, n_z), "z")
    both = jnp.concatenate([left, right], axis=1)
    input_grad = (both[:own] + fetch(both[own:].astype(BF), "x_lo", 1).astype(F32)).astype(BF)

    first = jnp.einsum("th,td->hd", both_grads, tok, preferred_element_type=F32)
    last = jnp.einsum("th,td->hd", hidden, grd, preferred_element_type=F32)
    first = scatter_weight_grads(first.reshape(2, hid, width)) * keep[:2].astype(F32)
    last = scatter_weight_grads(last[None]) * keep[2:].astype(F32)
    return (input_grad, first[0].astype(BF), first[1].astype(BF), last[0].astype(BF))


def solution(mesh):
    fine = Mesh(mesh.devices.reshape(SIZES), AXES)
    rows = P(DP + MP, None)
    weights = P(MP, DP)
    return jax.shard_map(
        per_device,
        mesh=fine,
        in_specs=(rows, rows, weights, weights, weights, P(), P(MP)),
        out_specs=(rows, weights, weights, weights),
        check_vma=False,
    )
```

```python
import jax
import jax.numpy as jnp
from jax import lax
from jax.experimental import pallas as pl
from jax.experimental.pallas import tpu as pltpu
from jax.sharding import Mesh
from jax.sharding import PartitionSpec as P

BLK = 128
AXES = ("x_hi", "core", "x_lo", "y", "z")
SIZES = (2, 2, 2, 4, 8)
DP = ("x_hi", "core")
MP = ("x_lo", "y", "z")
N_X, N_Y, N_Z = 2, 4, 8
BF = jnp.bfloat16
F32 = jnp.float32
WHOLE = pl.BlockSpec(memory_space=pltpu.VMEM)
SCALARS = pl.BlockSpec(memory_space=pltpu.SMEM)


def call(kernel, out_shape, in_specs, bytes_accessed, flops=0, **more):
    return pl.pallas_call(
        kernel,
        out_shape=out_shape,
        in_specs=in_specs,
        compiler_params=pltpu.CompilerParams(vmem_limit_bytes=(8 << 20) + 2 * bytes_accessed),
        cost_estimate=pl.CostEstimate(
            flops=flops, bytes_accessed=bytes_accessed, transcendentals=0
        ),
        **more,
    )


def fetch(block, axis, offset):
    size = SIZES[AXES.index(axis)]
    return lax.ppermute(block, axis, [(i, (i - offset) % size) for i in range(size)])


def pack(arrays):
    own, width = arrays[0].shape
    tail, rows = width // (own - 1), own - 1

    def kernel(*refs):
        out = refs[-1]
        for k, ref in enumerate(refs[:-1]):
            out[k * rows : (k + 1) * rows, :width] = ref[:rows, :]
            for i in range(rows):
                spot = k * rows + i
                out[spot : spot + 1, width:] = ref[rows : rows + 1, i * tail : (i + 1) * tail]

    out = jax.ShapeDtypeStruct((rows * len(arrays), width + tail), BF)
    return call(kernel, out, [WHOLE] * len(arrays), 4 * own * width * len(arrays))(*arrays)


def by_array(mine, other):
    rows = mine.shape[0] // 2

    def kernel(mine_ref, other_ref, *out):
        for k in range(2):
            out[k][:rows, :] = mine_ref[k * rows : (k + 1) * rows, :]
            out[k][rows:, :] = other_ref[k * rows : (k + 1) * rows, :]

    out = [jax.ShapeDtypeStruct(mine.shape, BF)] * 2
    return call(kernel, out, [WHOLE] * 2, 4 * mine.shape[0] * mine.shape[1])(mine, other)


def stack(blocks):
    starts = [sum(b.shape[0] for b in blocks[:i]) for i in range(len(blocks) + 1)]

    def kernel(*refs):
        for ref, start in zip(refs[:-1], starts):
            refs[-1][start : start + ref.shape[0], :] = ref[...]

    whole = jax.ShapeDtypeStruct((starts[-1], blocks[0].shape[1]), blocks[0].dtype)
    size = 4 * starts[-1] * blocks[0].shape[1]
    return call(kernel, whole, [WHOLE] * len(blocks), size)(*blocks)


def beside(parts):
    rows, cols = parts[0].shape

    def kernel(left, right, out):
        out[:, :cols] = left[...]
        out[:, cols:] = right[...]

    out = jax.ShapeDtypeStruct((rows, 2 * cols), parts[0].dtype)
    return call(kernel, out, [WHOLE] * 2, 8 * rows * cols)(*parts)


def unpack(pieces, units, own, width):
    tail = width // (own - 1)
    flat = [block for _, blocks in pieces for block in blocks]

    def kernel(*refs):
        out, at = refs[-1], 0
        for firsts, blocks in pieces:
            held = refs[at : at + len(blocks)]
            at += len(blocks)
            for i, unit in enumerate(firsts):
                rows = slice(8 * i, 8 * i + 8)
                top = unit * own
                value = jnp.concatenate([ref[rows, :] for ref in held], axis=1)
                out[top : top + own - 1, :] = value[:, :width]
                for j in range(own - 1):
                    part = value[j : j + 1, width:]
                    out[top + own - 1 : top + own, j * tail : (j + 1) * tail] = part

    whole = jax.ShapeDtypeStruct((units * own, width), BF)
    return call(kernel, whole, [WHOLE] * len(flat), 4 * units * own * width)(*flat)


def mask_weights(weights, keep_rows):
    rows, cols = weights[0].shape
    panels = rows // BLK

    def kernel(keep_ref, *refs):
        for m in range(len(weights)):
            for p in range(panels):
                row = m * panels + p
                keep = keep_ref[row : row + 1, :]
                kept = refs[m][p * BLK : (p + 1) * BLK, :].astype(F32) * keep
                refs[-1][row * BLK : (row + 1) * BLK, :] = kept.astype(BF)

    out = jax.ShapeDtypeStruct((rows * len(weights), cols), BF)
    return call(kernel, out, [WHOLE] * 4, 12 * rows * cols)(keep_rows, *weights)


def project(place, rows_in, blocks, row_block, count):
    total, width = rows_in.shape
    cols = width // 4

    def kernel(place_ref, x_ref, *refs):
        out = refs[-1]
        for b in range(4):

            @pl.when(pl.program_id(0) == b)
            def _():
                part = lax.dot_general(
                    x_ref[...], refs[b][...], (((1,), (1,)), ((), ())), preferred_element_type=F32
                )
                out[...] = part if b == 0 else out[...] + part

    return pl.pallas_call(
        kernel,
        grid_spec=pltpu.PrefetchScalarGridSpec(
            num_scalar_prefetch=1,
            grid=(4,),
            in_specs=[pl.BlockSpec((total, cols), lambda j, place: (0, place[j]))]
            + [pl.BlockSpec((count, cols), lambda j, place: (row_block, 0))] * 4,
            out_specs=pl.BlockSpec((total, count), lambda j, place: (0, 0)),
        ),
        out_shape=jax.ShapeDtypeStruct((total, count), F32),
        compiler_params=pltpu.CompilerParams(vmem_limit_bytes=24 << 20),
        cost_estimate=pl.CostEstimate(
            flops=2 * total * count * width,
            bytes_accessed=2 * total * width + 2 * count * width + 4 * total * count,
            transcendentals=0,
        ),
    )(place, rows_in, *blocks)


def spread(grads, blocks):
    total, count = grads.shape
    cols, n = blocks[0].shape[1], len(blocks)

    def kernel(g_ref, *refs):
        for j in range(n):

            @pl.when(pl.program_id(0) == j)
            def _():
                part = jnp.dot(g_ref[...], refs[j][...], preferred_element_type=F32)
                refs[-1][...] = part.astype(BF)

    return pl.pallas_call(
        kernel,
        grid=(n,),
        in_specs=[pl.BlockSpec((total, count), lambda j: (0, 0))]
        + [pl.BlockSpec((count, cols), lambda j: (0, 0))] * n,
        out_specs=pl.BlockSpec((total, cols), lambda j: (0, j)),
        out_shape=jax.ShapeDtypeStruct((total, n * cols), BF),
        compiler_params=pltpu.CompilerParams(vmem_limit_bytes=24 << 20),
        cost_estimate=pl.CostEstimate(
            flops=2 * n * total * count * cols,
            bytes_accessed=2 * n * cols * (total + count),
            transcendentals=0,
        ),
    )(grads, *blocks)


def deal(total, unit):
    count = total.shape[0] // unit

    def kernel(ref, *out):
        for i in range(count):
            out[i][...] = ref[i * unit : (i + 1) * unit, :]

    spec = [jax.ShapeDtypeStruct((unit, total.shape[1]), BF)] * count
    return call(kernel, spec, [WHOLE], 6 * total.shape[0] * total.shape[1])(total)


def activations(z, pre, hidden_grad, unit):
    total, hid = hidden_grad.shape
    block = N_Y * unit

    def kernel(z_ref, pre_ref, grad_ref, first_ref, hidden_ref):
        for dz in range(N_Z):
            spot = lax.rem(z_ref[0] + dz, N_Z)
            gate_pre, up_pre = pre_ref[spot, :, :hid], pre_ref[spot, :, hid:]
            rows = [slice((dy * N_Z + dz) * unit, (dy * N_Z + dz + 1) * unit) for dy in range(N_Y)]
            grad = jnp.concatenate([grad_ref[r, :] for r in rows], axis=0)
            sigma = jax.nn.sigmoid(gate_pre)
            swish = gate_pre * sigma
            hidden = (swish * up_pre).astype(BF)
            up_grad = (grad * swish).astype(BF)
            gate_grad = (grad * up_pre * sigma * (1.0 + gate_pre * (1.0 - sigma))).astype(BF)
            first_ref[spot, :, :hid] = gate_grad
            first_ref[spot, :, hid:] = up_grad
            for dy in range(N_Y):
                part = slice(dy * unit, (dy + 1) * unit)
                hidden_ref[rows[dy], :] = hidden[part]

    out = [
        jax.ShapeDtypeStruct((N_Z, block, 2 * hid), BF),
        jax.ShapeDtypeStruct((total, hid), BF),
    ]
    first, hidden = call(kernel, out, [SCALARS] + [WHOLE] * 2, 16 * total * hid)(
        z, pre.reshape(N_Z, block, 2 * hid), hidden_grad
    )
    return first.reshape(total, 2 * hid), hidden


def weight_grads(order, left, right):
    tokens, hid = left.shape
    cols = right.shape[1] // 4

    def kernel(order_ref, left_ref, right_ref, give_ref, keep_ref):
        part = lax.dot_general(
            left_ref[...], right_ref[...], (((0,), (0,)), ((), ())), preferred_element_type=F32
        )

        @pl.when(pl.program_id(0) < 2)
        def _():
            give_ref[0] = part.astype(BF)

        @pl.when(pl.program_id(0) >= 2)
        def _():
            keep_ref[0] = part

    return pl.pallas_call(
        kernel,
        grid_spec=pltpu.PrefetchScalarGridSpec(
            num_scalar_prefetch=1,
            grid=(4,),
            in_specs=[
                pl.BlockSpec((tokens, hid), lambda j, order: (0, 0)),
                pl.BlockSpec((tokens, cols), lambda j, order: (0, order[j])),
            ],
            out_specs=[
                pl.BlockSpec((1, hid, cols), lambda j, order: (jnp.minimum(j, 1), 0, 0)),
                pl.BlockSpec((1, hid, cols), lambda j, order: (jnp.maximum(j - 2, 0), 0, 0)),
            ],
        ),
        out_shape=[
            jax.ShapeDtypeStruct((2, hid, cols), BF),
            jax.ShapeDtypeStruct((2, hid, cols), F32),
        ],
        compiler_params=pltpu.CompilerParams(vmem_limit_bytes=24 << 20),
        cost_estimate=pl.CostEstimate(
            flops=8 * tokens * hid * cols,
            bytes_accessed=12 * hid * cols + 8 * tokens * cols,
            transcendentals=0,
        ),
    )(order, left, right)


def per_device(tokens, out_grad, gate_weight, up_weight, down_weight, block_mask, assignment):
    own, width = tokens.shape
    hid, cols = gate_weight.shape
    panels, col_blocks = hid // BLK, cols // BLK
    unit = 2 * own
    x_hi, core, z = (lax.axis_index(a) for a in ("x_hi", "core", "z"))
    place = jnp.stack(
        [2 * x_hi + core, 2 * (1 - x_hi) + core, 2 * x_hi + 1 - core, 2 * (1 - x_hi) + 1 - core]
    )
    tie = lax.optimization_barrier

    panel_ids = lax.broadcasted_iota(jnp.int32, (panels, block_mask.shape[1]), 1)
    selector = (assignment[:, None] == panel_ids).astype(F32)
    slot_mask = jnp.einsum("sp,mpb->msb", selector, block_mask.astype(F32))
    slot_mask = lax.dynamic_slice_in_dim(slot_mask, place[0] * col_blocks, col_blocks, 2)
    keep = jnp.repeat(slot_mask, BLK, axis=2)

    mine = pack([tokens, out_grad])
    tok16, grd16 = by_array(mine, fetch(mine, "x_lo", 1))
    kept = mask_weights([gate_weight, up_weight, down_weight], keep.reshape(-1, cols))
    tok16, grd16, kept = tie((tok16, grd16, kept))

    away = fetch(kept, "x_hi", 1)
    z1, z7 = fetch(grd16, "z", 1), fetch(grd16, "z", -1)
    t1, t3, t2 = fetch(tok16, "y", 1), fetch(tok16, "y", -1), fetch(tok16, "y", 2)
    z1, z7, t1, t3, t2 = tie((z1, z7, t1, t3, t2))
    tok = unpack(
        [([2 * dy, 2 * dy + 1], [t]) for dy, t in enumerate((tok16, t1, t2, t3))], N_X * N_Y, own, width
    )
    tok = lax.all_gather(tok, "z", axis=0, tiled=True)
    near = stack([grd16, z1, z7])
    z2, z6, n1, n3 = tie(
        (fetch(z1, "z", 1), fetch(z7, "z", -1), fetch(near, "y", 1), fetch(near, "y", -1))
    )
    cut = near.shape[1] // 2
    z3, z5, n2a, n2b = tie(
        (
            fetch(z2, "z", 1),
            fetch(z6, "z", -1),
            fetch(n1[:, :cut], "y", 1),
            fetch(n3[:, cut:], "y", -1),
        )
    )
    z4 = beside(tie((fetch(z3[:, :cut], "z", 1), fetch(z5[:, cut:], "z", -1))))
    rest = stack([z2, z3, z4, z5, z6])
    r1, r3, away = tie((fetch(rest, "y", 1), fetch(rest, "y", -1), away))
    beside_kept, beside_away = fetch(kept, "core", 1), fetch(away, "core", 1)
    r2a, r2b = fetch(r1[:, :cut], "y", 1), fetch(r3[:, cut:], "y", -1)
    pieces = []
    for dy, n, r in ((0, [near], [rest]), (1, [n1], [r1]), (2, [n2a, n2b], [r2a, r2b]), (3, [n3], [r3])):
        for offsets, blocks in (((0, 1, 7), n), ((2, 3, 4, 5, 6), r)):
            pieces.append(([2 * (N_Z * dy + dz) + dx for dz in offsets for dx in range(N_X)], blocks))
    grd = unpack(pieces, N_X * N_Y * N_Z, own, width)

    blocks = [kept, away, beside_kept, beside_away]
    hidden_grad = project(place, grd, blocks, 2, hid)
    pre = project(place, tok, blocks, 0, 2 * hid)
    by_z, hidden = activations(z[None], pre, hidden_grad, unit)

    total = spread(by_z, blocks)
    total = lax.psum_scatter(total, "z", scatter_dimension=0, tiled=True)
    order = place[::-1]
    give_b, keep_b = weight_grads(order, hidden, grd)
    give_b = fetch(give_b, "core", 1)
    give_a, keep_a = weight_grads(order, by_z, tok)
    give_a, give_b, keep_a = tie((give_a, give_b, keep_a))
    sums_b = keep_b + give_b.astype(F32)
    far_b = fetch(sums_b[0].astype(BF), "x_hi", 1)
    sums_a = keep_a + fetch(give_a, "core", 1).astype(F32)
    far_a = fetch(sums_a[0].astype(BF), "x_hi", 1)

    parts = deal(total, unit)
    parts = [parts[0]] + [fetch(parts[dy], "y", -dy) for dy in range(1, N_Y)]
    both = sum(part.astype(F32) for part in parts)
    both = both[:own] + fetch(both[own:].astype(BF), "x_lo", 1).astype(F32)
    quarters = [both[:, i * cols : (i + 1) * cols] for i in (0, 2, 1, 3)]
    quarters = [jnp.where(core == 0, quarters[i], quarters[i ^ 1]) for i in range(4)]
    quarters = [jnp.where(x_hi == 0, quarters[i], quarters[i ^ 2]) for i in range(4)]
    input_grad = jnp.concatenate(quarters, axis=1).astype(BF)

    def finish(sums, far, rows):
        total = (sums[1] + far.astype(F32)).reshape(-1, panels, BLK, cols)
        return (total * rows[:, :, None, :]).astype(BF).reshape(-1, hid, cols)

    gate_up_grad = finish(sums_a, far_a, keep[:2])
    down_grad = finish(sums_b, far_b, keep[2:])
    return (input_grad, gate_up_grad[0], gate_up_grad[1], down_grad[0])


def solution(mesh):
    fine = Mesh(mesh.devices.reshape(SIZES), AXES)
    rows = P(DP + MP, None)
    weights = P(MP, DP)
    return jax.shard_map(
        per_device,
        mesh=fine,
        in_specs=(rows, rows, weights, weights, weights, P(), P(MP)),
        out_specs=(rows, weights, weights, weights),
        check_vma=False,
    )
```

```python
import jax
import jax.numpy as jnp
from jax import lax
from jax.experimental import pallas as pl
from jax.experimental.pallas import tpu as pltpu
from jax.sharding import Mesh
from jax.sharding import PartitionSpec as P

BLK = 128
AXES = ("x_hi", "core", "x_lo", "y", "z")
SIZES = (2, 2, 2, 4, 8)
DP = ("x_hi", "core")
MP = ("x_lo", "y", "z")
N_X, N_Y, N_Z = 2, 4, 8
BF = jnp.bfloat16
F32 = jnp.float32
WHOLE = pl.BlockSpec(memory_space=pltpu.VMEM)
VMEM_LIMIT = 6 << 20
BIG_LIMIT = 52 << 20
ANYWHERE = pl.BlockSpec(memory_space=pl.ANY)
SCALARS = pl.BlockSpec(memory_space=pltpu.SMEM)


def call(kernel, out_shape, in_specs, bytes_accessed, flops=0, **more):
    return pl.pallas_call(
        kernel,
        out_shape=out_shape,
        in_specs=in_specs,
        out_specs=more.pop("out_specs", jax.tree.map(lambda _: WHOLE, out_shape)),
        compiler_params=pltpu.CompilerParams(vmem_limit_bytes=more.pop("limit", VMEM_LIMIT)),
        cost_estimate=pl.CostEstimate(
            flops=flops, bytes_accessed=bytes_accessed, transcendentals=0
        ),
        **more,
    )


def local(function, *arrays):
    out = jax.eval_shape(function, *arrays)

    def kernel(*refs):
        results = function(*(ref[...] for ref in refs[: len(arrays)]))
        for ref, value in zip(refs[len(arrays) :], results):
            ref[...] = value

    size = sum(a.size * a.dtype.itemsize for a in (*arrays, *out))
    return call(kernel, list(out), [WHOLE] * len(arrays), size)(*arrays)


def fetch(block, axis, offset):
    size = SIZES[AXES.index(axis)]
    return lax.ppermute(block, axis, [(i, (i - offset) % size) for i in range(size)])


def pack(arrays):
    own, width = arrays[0].shape
    tail, rows = width // (own - 1), own - 1

    def kernel(*refs):
        out = refs[-1]
        for k, ref in enumerate(refs[:-1]):
            out[k * rows : (k + 1) * rows, :width] = ref[:rows, :]
            for i in range(rows):
                spot = k * rows + i
                out[spot : spot + 1, width:] = ref[rows : rows + 1, i * tail : (i + 1) * tail]

    out = jax.ShapeDtypeStruct((rows * len(arrays), width + tail), BF)
    return call(kernel, out, [WHOLE] * len(arrays), 4 * own * width * len(arrays))(*arrays)


def by_array(mine, other):
    rows = mine.shape[0] // 2

    def kernel(mine_ref, other_ref, *out):
        for k in range(2):
            out[k][:rows, :] = mine_ref[k * rows : (k + 1) * rows, :]
            out[k][rows:, :] = other_ref[k * rows : (k + 1) * rows, :]

    out = [jax.ShapeDtypeStruct(mine.shape, BF)] * 2
    return call(kernel, out, [WHOLE] * 2, 4 * mine.shape[0] * mine.shape[1])(mine, other)


def stack(blocks):
    starts = [sum(b.shape[0] for b in blocks[:i]) for i in range(len(blocks) + 1)]

    def kernel(*refs):
        for ref, start in zip(refs[:-1], starts):
            refs[-1][start : start + ref.shape[0], :] = ref[...]

    whole = jax.ShapeDtypeStruct((starts[-1], blocks[0].shape[1]), blocks[0].dtype)
    size = 4 * starts[-1] * blocks[0].shape[1]
    return call(kernel, whole, [WHOLE] * len(blocks), size)(*blocks)


def join(lines):
    spots, flat, top = [], [], 0
    for line in lines:
        left = 0
        for block in line:
            spots.append((top, left))
            flat.append(block)
            left += block.shape[1]
        top += line[0].shape[0]

    def kernel(*refs):
        for ref, (row, col) in zip(refs[:-1], spots):
            refs[-1][row : row + ref.shape[0], col : col + ref.shape[1]] = ref[...]

    whole = jax.ShapeDtypeStruct((top, left), flat[0].dtype)
    return call(kernel, whole, [WHOLE] * len(flat), 4 * top * left)(*flat)


def unpack(pieces, units, own, width):
    tail = width // (own - 1)
    flat = [block for _, blocks in pieces for block in blocks]

    def kernel(*refs):
        out, at = refs[-1], 0
        for firsts, blocks in pieces:
            held = refs[at : at + len(blocks)]
            at += len(blocks)
            for i, unit in enumerate(firsts):
                rows = slice(8 * i, 8 * i + 8)
                top = unit * own
                value = jnp.concatenate([ref[rows, :] for ref in held], axis=1)
                out[top : top + own - 1, :] = value[:, :width]
                for j in range(own - 1):
                    part = value[j : j + 1, width:]
                    out[top + own - 1 : top + own, j * tail : (j + 1) * tail] = part

    whole = jax.ShapeDtypeStruct((units * own, width), BF)
    return call(kernel, whole, [WHOLE] * len(flat), 4 * units * own * width)(*flat)


def mask_weights(weights, keep_rows):
    rows, cols = weights[0].shape
    panels = rows // BLK

    def kernel(keep_ref, *refs):
        for m in range(len(weights)):
            for p in range(panels):
                row = m * panels + p
                keep = keep_ref[row : row + 1, :]
                kept = refs[m][p * BLK : (p + 1) * BLK, :].astype(F32) * keep
                refs[-1][row * BLK : (row + 1) * BLK, :] = kept.astype(BF)

    out = jax.ShapeDtypeStruct((rows * len(weights), cols), BF)
    return call(kernel, out, [WHOLE] * 4, 12 * rows * cols)(keep_rows, *weights)


def turn(array):
    return local(lambda a: (a.T,), array)[0]


def deal(total, unit):
    count = total.shape[0] // unit

    def kernel(ref, *out):
        for i in range(count):
            out[i][...] = ref[i * unit : (i + 1) * unit, :]

    spec = [jax.ShapeDtypeStruct((unit, total.shape[1]), BF)] * count
    return call(kernel, spec, [WHOLE], 6 * total.shape[0] * total.shape[1])(total)


def place_rows(place, mine, other):
    rows, width = mine.shape
    cols = width // 4

    def kernel(place_ref, mine_ref, other_ref, out):
        for b in range(4):
            held = slice(b * cols, (b + 1) * cols)
            where = pl.ds(pl.multiple_of(place_ref[b] * cols, cols), cols)
            out[:, where] = (mine_ref[:, held] + other_ref[:, held]).astype(BF)

    out = jax.ShapeDtypeStruct((rows, width), BF)
    return call(kernel, out, [SCALARS, WHOLE, WHOLE], 10 * rows * width)(place, mine, other)


def middle(z, place, tok, pieces, turned, blocks, own):
    total, width = tok.shape
    hid, cols = blocks[0].shape[0] // 3, width // 4
    unit, tail = N_X * own, width // (own - 1)
    block = N_Y * unit
    flat = [part for _, held in pieces for part in held]
    n, m = len(flat), len(pieces)

    def kernel(z_ref, place_ref, tok_ref, *refs):
        piece_refs, turned_refs, block_refs = refs[:n], refs[n : n + 4], refs[n + 4 : n + 8]
        first_ref, grd_out, hidden_ref, out = refs[n + 8 : n + 12]
        packed = refs[n + 12 : n + 12 + m]
        x, wt, w, grd, g, pre, by_z, held, sems, out_sems = refs[n + 12 + m :]

        def bring(source, target, i):
            copy = pltpu.make_async_copy(source, target, sems.at[i])
            copy.start()
            return copy

        def spot(dz):
            return lax.rem(z_ref[0] + dz, N_Z)

        def at(b):
            return pl.ds(pl.multiple_of(place_ref[b] * cols, cols), cols)

        come, i = [], 0
        for target, (_, parts) in zip(packed, pieces):
            size = target.shape[1] // len(parts)
            for j in range(len(parts)):
                come.append(bring(piece_refs[i], target.at[:, j * size : (j + 1) * size], i))
                i += 1
        come_wt = [bring(turned_refs[b], wt.at[b], n + b) for b in range(4)]
        come_x = [bring(tok_ref.at[:, at(b)], x.at[b], n + 4 + b) for b in range(4)]
        come_w = [bring(block_refs[b].at[: 2 * hid, :], w.at[b], n + 8 + b) for b in range(4)]
        for copy in come:
            copy.wait()
        for source, (firsts, _) in zip(packed, pieces):
            for i, first in enumerate(firsts):
                value = source[8 * i : 8 * i + 8, :]
                top = first * own
                grd[top : top + own - 1, :] = value[:, :width]
                for j in range(own - 1):
                    part = value[j : j + 1, width:]
                    grd[top + own - 1 : top + own, j * tail : (j + 1) * tail] = part
        gone = [pltpu.make_async_copy(grd, grd_out, sems.at[0])]
        gone[0].start()
        acc = None
        for b in range(4):
            come_wt[b].wait()
            part = jnp.dot(grd[:, at(b)], wt[b, :, 2 * hid :], preferred_element_type=F32)
            acc = part if b == 0 else acc + part
        g[...] = acc
        for b in range(4):
            come_x[b].wait()
            part = jnp.dot(x[b], wt[b, :, : 2 * hid], preferred_element_type=F32)
            acc = part if b == 0 else acc + part
        for i in range(N_Z):
            pre[i] = acc[i * block : (i + 1) * block]
        for dz in range(N_Z):
            gate_pre, up_pre = pre[spot(dz), :, :hid], pre[spot(dz), :, hid:]
            rows = [slice((dy * N_Z + dz) * unit, (dy * N_Z + dz + 1) * unit) for dy in range(N_Y)]
            grad = jnp.concatenate([g[r, :] for r in rows], axis=0)
            sigma = jax.nn.sigmoid(gate_pre)
            swish = gate_pre * sigma
            hidden = (swish * up_pre).astype(BF)
            up_grad = (grad * swish).astype(BF)
            gate_grad = (grad * up_pre * sigma * (1.0 + gate_pre * (1.0 - sigma))).astype(BF)
            both = jnp.concatenate([gate_grad, up_grad], axis=1)
            first_ref[spot(dz)] = both
            by_z[dz * block : (dz + 1) * block, :] = both
            for dy in range(N_Y):
                hidden_ref[rows[dy], :] = hidden[dy * unit : (dy + 1) * unit]
        for b in range(4):
            come_w[b].wait()
            part = jnp.dot(by_z[...], w[b], preferred_element_type=F32).astype(BF)
            for dz in range(N_Z):
                held[b, dz] = part[dz * block : (dz + 1) * block]
                there = out.at[spot(dz), :, b * cols : (b + 1) * cols]
                gone.append(pltpu.make_async_copy(held.at[b, dz], there, out_sems.at[b, dz]))
                gone[-1].start()
        for copy in gone:
            copy.wait()

    first, grd, hidden, sums = call(
        kernel,
        [
            jax.ShapeDtypeStruct((N_Z, block, 2 * hid), BF),
            jax.ShapeDtypeStruct((total, width), BF),
            jax.ShapeDtypeStruct((total, hid), BF),
            jax.ShapeDtypeStruct((N_Z, block, width), BF),
        ],
        [SCALARS] * 2 + [ANYWHERE] * (n + 9),
        8 * total * width + 12 * hid * width,
        flops=10 * total * hid * width,
        limit=BIG_LIMIT,
        out_specs=[WHOLE, ANYWHERE, WHOLE, ANYWHERE],
        scratch_shapes=[
            pltpu.VMEM((8 * len(firsts), width + tail), BF) for firsts, _ in pieces
        ]
        + [
            pltpu.VMEM((4, total, cols), BF),
            pltpu.VMEM((4, cols, 3 * hid), BF),
            pltpu.VMEM((4, 2 * hid, cols), BF),
            pltpu.VMEM((total, width), BF),
            pltpu.VMEM((total, hid), F32),
            pltpu.VMEM((N_Z, block, 2 * hid), F32),
            pltpu.VMEM((total, 2 * hid), BF),
            pltpu.VMEM((4, N_Z, block, cols), BF),
            pltpu.SemaphoreType.DMA((n + 12,)),
            pltpu.SemaphoreType.DMA((4, N_Z)),
        ],
    )(z, place, tok, *flat, *turned, *blocks)
    return first.reshape(total, 2 * hid), grd, hidden, sums.reshape(total, width)


def weight_grads(order, lefts, rights):
    hid, cols, n = lefts[0].shape[1], rights[0].shape[1] // 4, len(lefts)
    rows = lefts[0].shape[0]

    def kernel(order_ref, *refs):
        give_ref, keep_ref, held, sems = refs[2 * n :]
        come = {}
        for b in range(4):
            where = pl.ds(pl.multiple_of(order_ref[b] * cols, cols), cols)
            for i, right in enumerate(refs[n : 2 * n]):
                there = held.at[b, i * rows : (i + 1) * rows, :]
                come[b, i] = pltpu.make_async_copy(right.at[:, where], there, sems.at[b, i])
                come[b, i].start()
        left = jnp.concatenate([ref[...] for ref in refs[:n]], axis=0).T
        for b in range(4):
            for i in range(n):
                come[b, i].wait()
            part = jnp.dot(left, held[b], preferred_element_type=F32)
            if b < 2:
                give_ref[b] = part.astype(BF)
            else:
                keep_ref[b - 2] = part

    return call(
        kernel,
        [jax.ShapeDtypeStruct((2, hid, cols), BF), jax.ShapeDtypeStruct((2, hid, cols), F32)],
        [SCALARS] + [WHOLE] * n + [ANYWHERE] * n,
        12 * hid * cols + 8 * n * rows * cols,
        flops=8 * n * rows * hid * cols,
        limit=BIG_LIMIT,
        scratch_shapes=[
            pltpu.VMEM((4, n * rows, cols), BF),
            pltpu.SemaphoreType.DMA((4, n)),
        ],
    )(order, *lefts, *rights)


def per_device(tokens, out_grad, gate_weight, up_weight, down_weight, block_mask, assignment):
    own, width = tokens.shape
    hid, cols = gate_weight.shape
    panels, col_blocks = hid // BLK, cols // BLK
    unit = 2 * own
    x_hi, core, z = (lax.axis_index(a) for a in ("x_hi", "core", "z"))
    place = jnp.stack(
        [2 * x_hi + core, 2 * (1 - x_hi) + core, 2 * x_hi + 1 - core, 2 * (1 - x_hi) + 1 - core]
    )
    tie = lax.optimization_barrier

    panel_ids = lax.broadcasted_iota(jnp.int32, (panels, block_mask.shape[1]), 1)
    selector = (assignment[:, None] == panel_ids).astype(F32)
    slot_mask = jnp.einsum("sp,mpb->msb", selector, block_mask.astype(F32))
    slot_mask = lax.dynamic_slice_in_dim(slot_mask, place[0] * col_blocks, col_blocks, 2)
    keep = jnp.repeat(slot_mask, BLK, axis=2)

    mine = pack([tokens, out_grad])
    tok16, grd16 = by_array(mine, fetch(mine, "x_lo", 1))
    kept = mask_weights([gate_weight, up_weight, down_weight], keep.reshape(-1, cols))
    tok16, grd16, kept = tie((tok16, grd16, kept))

    t1, t3, t2 = fetch(tok16, "y", 1), fetch(tok16, "y", -1), fetch(tok16, "y", 2)
    z1, z7 = fetch(grd16, "z", 1), fetch(grd16, "z", -1)
    z1, z7, t1, t3, t2 = tie((z1, z7, t1, t3, t2))
    tok = unpack(
        [([2 * dy, 2 * dy + 1], [t]) for dy, t in enumerate((tok16, t1, t2, t3))], N_X * N_Y, own, width
    )
    tok = lax.all_gather(tok, "z", axis=0, tiled=True)
    away = fetch(kept, "x_hi", 1)
    z2, z6, beside_kept = tie(
        (fetch(z1, "z", 1), fetch(z7, "z", -1), fetch(kept, "core", 1))
    )
    near = stack([grd16, z1, z7, z2, z6])
    cut = near.shape[1] // 2
    n1, n3 = fetch(near, "y", 1), fetch(near, "y", -1)
    z3, z5 = tie((fetch(z2, "z", 1), fetch(z6, "z", -1)))
    z4 = tie([fetch(z3[:, :cut], "z", 1), fetch(z5[:, cut:], "z", -1)])
    rest = join([[z3], [z5], z4])
    kept_turned, beside_turned = turn(kept), turn(beside_kept)
    n1, n3, rest, kept_turned, beside_turned = tie((n1, n3, rest, kept_turned, beside_turned))
    n2 = [fetch(n1[:, :cut], "y", 1), fetch(n3[:, cut:], "y", -1)]
    r1, r3 = fetch(rest, "y", 1), fetch(rest, "y", -1)
    n2, r1, r3, away = tie((n2, r1, r3, away))
    r2 = [fetch(r1[:, :cut], "y", 1), fetch(r3[:, cut:], "y", -1)]
    beside_away = fetch(away, "core", 1)
    blocks = [kept, away, beside_kept, beside_away]
    turned = [kept_turned, turn(away), beside_turned, turn(beside_away)]
    tok, r2, turned = tie((tok, r2, turned))
    pieces = []
    for dy, n, r in ((0, [near], [rest]), (1, [n1], [r1]), (2, n2, r2), (3, [n3], [r3])):
        for offsets, held in (((0, 1, 7, 2, 6), n), ((3, 5, 4), r)):
            pieces.append(([2 * (N_Z * dy + dz) + dx for dz in offsets for dx in range(N_X)], held))
    by_z, grd, hidden, total = middle(z[None], place, tok, pieces, turned, blocks, own)
    total = lax.psum_scatter(total, "z", scatter_dimension=0, tiled=True)

    order = place[::-1]
    give_a, keep_a = weight_grads(order, [by_z], [tok])
    give_a = fetch(give_a, "core", 1)
    give_b, keep_b = weight_grads(order, [hidden], [grd])
    give_a, give_b, keep_b = tie((give_a, give_b, keep_b))
    far_a = fetch((keep_a[0] + give_a[0].astype(F32)).astype(BF), "x_hi", 1)
    give_b = fetch(give_b, "core", 1)
    far_b = fetch((keep_b[0] + give_b[0].astype(F32)).astype(BF), "x_hi", 1)

    def finish(keep_sum, give, far, rows):
        total = keep_sum[1] + give[1].astype(F32) + far.astype(F32)
        total = total.reshape(-1, panels, BLK, cols) * rows[:, :, None, :]
        return total.astype(BF).reshape(-1, hid, cols)

    gate_up_grad = finish(keep_a, give_a, far_a, keep[:2])
    down_grad = finish(keep_b, give_b, far_b, keep[2:])

    parts = deal(total, unit)
    parts = [parts[0]] + [fetch(parts[dy], "y", -dy) for dy in (1, 3, 2)]

    def last(*parts):
        both = sum(part.astype(F32) for part in parts)
        return both[:own], both[own:]

    parts, gate_up_grad, down_grad = tie((parts, gate_up_grad, down_grad))
    mine, other = local(last, *parts)
    input_grad = place_rows(place, mine, fetch(other, "x_lo", 1))
    return (input_grad, gate_up_grad[0], gate_up_grad[1], down_grad[0])


def solution(mesh):
    fine = Mesh(mesh.devices.reshape(SIZES), AXES)
    rows = P(DP + MP, None)
    weights = P(MP, DP)
    return jax.shard_map(
        per_device,
        mesh=fine,
        in_specs=(rows, rows, weights, weights, weights, P(), P(MP)),
        out_specs=(rows, weights, weights, weights),
        check_vma=False,
    )
```

```python
import jax
import jax.numpy as jnp
from jax import lax
from jax.experimental import pallas as pl
from jax.experimental.pallas import tpu as pltpu
from jax.sharding import Mesh
from jax.sharding import PartitionSpec as P

BLK = 128
AXES = ("x_hi", "core", "x_lo", "y", "z")
SIZES = (2, 2, 2, 4, 8)
DP = ("x_hi", "core")
MP = ("x_lo", "y", "z")
N_X, N_Y, N_Z = 2, 4, 8
BF = jnp.bfloat16
F32 = jnp.float32
WHOLE = pl.BlockSpec(memory_space=pltpu.VMEM)
VMEM_LIMIT = 6 << 20
BIG_LIMIT = 52 << 20
ANYWHERE = pl.BlockSpec(memory_space=pl.ANY)
SCALARS = pl.BlockSpec(memory_space=pltpu.SMEM)


def call(kernel, out_shape, in_specs, bytes_accessed, flops=0, **more):
    return pl.pallas_call(
        kernel,
        out_shape=out_shape,
        in_specs=in_specs,
        out_specs=more.pop("out_specs", jax.tree.map(lambda _: WHOLE, out_shape)),
        compiler_params=pltpu.CompilerParams(vmem_limit_bytes=more.pop("limit", VMEM_LIMIT)),
        cost_estimate=pl.CostEstimate(
            flops=flops, bytes_accessed=bytes_accessed, transcendentals=0
        ),
        **more,
    )


def local(function, *arrays):
    out = jax.eval_shape(function, *arrays)

    def kernel(*refs):
        results = function(*(ref[...] for ref in refs[: len(arrays)]))
        for ref, value in zip(refs[len(arrays) :], results):
            ref[...] = value

    size = sum(a.size * a.dtype.itemsize for a in (*arrays, *out))
    return call(kernel, list(out), [WHOLE] * len(arrays), size)(*arrays)


def fetch(block, axis, offset):
    size = SIZES[AXES.index(axis)]
    return lax.ppermute(block, axis, [(i, (i - offset) % size) for i in range(size)])


def pack(arrays):
    own, width = arrays[0].shape
    tail, rows = width // (own - 1), own - 1

    def kernel(*refs):
        out = refs[-1]
        for k, ref in enumerate(refs[:-1]):
            out[k * rows : (k + 1) * rows, :width] = ref[:rows, :]
            for i in range(rows):
                spot = k * rows + i
                out[spot : spot + 1, width:] = ref[rows : rows + 1, i * tail : (i + 1) * tail]

    out = jax.ShapeDtypeStruct((rows * len(arrays), width + tail), BF)
    return call(kernel, out, [WHOLE] * len(arrays), 4 * own * width * len(arrays))(*arrays)


def by_array(mine, other):
    rows = mine.shape[0] // 2

    def kernel(mine_ref, other_ref, *out):
        for k in range(2):
            out[k][:rows, :] = mine_ref[k * rows : (k + 1) * rows, :]
            out[k][rows:, :] = other_ref[k * rows : (k + 1) * rows, :]

    out = [jax.ShapeDtypeStruct(mine.shape, BF)] * 2
    return call(kernel, out, [WHOLE] * 2, 4 * mine.shape[0] * mine.shape[1])(mine, other)


def stack(blocks):
    starts = [sum(b.shape[0] for b in blocks[:i]) for i in range(len(blocks) + 1)]

    def kernel(*refs):
        for ref, start in zip(refs[:-1], starts):
            refs[-1][start : start + ref.shape[0], :] = ref[...]

    whole = jax.ShapeDtypeStruct((starts[-1], blocks[0].shape[1]), blocks[0].dtype)
    size = 4 * starts[-1] * blocks[0].shape[1]
    return call(kernel, whole, [WHOLE] * len(blocks), size)(*blocks)


def join(lines):
    spots, flat, top = [], [], 0
    for line in lines:
        left = 0
        for block in line:
            spots.append((top, left))
            flat.append(block)
            left += block.shape[1]
        top += line[0].shape[0]

    def kernel(*refs):
        for ref, (row, col) in zip(refs[:-1], spots):
            refs[-1][row : row + ref.shape[0], col : col + ref.shape[1]] = ref[...]

    whole = jax.ShapeDtypeStruct((top, left), flat[0].dtype)
    return call(kernel, whole, [WHOLE] * len(flat), 4 * top * left)(*flat)


def unpack(pieces, units, own, width):
    tail = width // (own - 1)
    flat = [block for _, blocks in pieces for block in blocks]

    def kernel(*refs):
        out, at = refs[-1], 0
        for firsts, blocks in pieces:
            held = refs[at : at + len(blocks)]
            at += len(blocks)
            for i, unit in enumerate(firsts):
                rows = slice(8 * i, 8 * i + 8)
                top = unit * own
                value = jnp.concatenate([ref[rows, :] for ref in held], axis=1)
                out[top : top + own - 1, :] = value[:, :width]
                for j in range(own - 1):
                    part = value[j : j + 1, width:]
                    out[top + own - 1 : top + own, j * tail : (j + 1) * tail] = part

    whole = jax.ShapeDtypeStruct((units * own, width), BF)
    return call(kernel, whole, [WHOLE] * len(flat), 4 * units * own * width)(*flat)


def mask_weights(weights, keep_rows):
    rows, cols = weights[0].shape
    panels = rows // BLK

    def kernel(keep_ref, *refs):
        for m in range(len(weights)):
            for p in range(panels):
                row = m * panels + p
                keep = keep_ref[row : row + 1, :]
                kept = refs[m][p * BLK : (p + 1) * BLK, :].astype(F32) * keep
                half, row = divmod(row, len(weights) * panels // 2)
                refs[half - 2][row * BLK : (row + 1) * BLK, :] = kept.astype(BF)

    out = [jax.ShapeDtypeStruct((rows * len(weights) // 2, cols), BF)] * 2
    return call(kernel, out, [WHOLE] * 4, 12 * rows * cols)(keep_rows, *weights)


def turn(halves):
    rows, cols = halves[0].shape

    def kernel(top, bottom, out):
        out[:, :rows] = top[...].T
        out[:, rows:] = bottom[...].T

    out = jax.ShapeDtypeStruct((cols, 2 * rows), BF)
    return call(kernel, out, [WHOLE] * 2, 8 * rows * cols)(*halves)


def deal(total, own):
    width = total.shape[1]
    unit, rows, tail = N_X * own, own - 1, width // (own - 1)
    count = total.shape[0] // unit

    def kernel(ref, *out):
        for u in range(count):
            for k in range(N_X):
                top = u * unit + k * own
                out[u][k * rows : (k + 1) * rows, :width] = ref[top : top + rows, :]
                for i in range(rows):
                    part = ref[top + rows : top + own, i * tail : (i + 1) * tail]
                    out[u][k * rows + i : k * rows + i + 1, width:] = part

    spec = [jax.ShapeDtypeStruct((N_X * rows, width + tail), BF)] * count
    return call(kernel, spec, [WHOLE], 6 * total.shape[0] * width)(total)


def place_rows(place, mine, other):
    rows, packed = mine.shape
    width = packed * rows // (rows + 1)
    cols, tail = width // 4, width // rows

    def kernel(place_ref, mine_ref, other_ref, out):
        total = (mine_ref[...] + other_ref[...]).astype(BF)
        for b in range(4):
            start = place_ref[b] * cols
            where = pl.ds(pl.multiple_of(start, tail), cols)
            out[:rows, where] = total[:, b * cols : (b + 1) * cols]
            for j in range(cols // tail):
                i = b * (cols // tail) + j
                where = pl.ds(pl.multiple_of(start + j * tail, tail), tail)
                out[rows : rows + 1, where] = total[i : i + 1, width:]

    out = jax.ShapeDtypeStruct((rows + 1, width), BF)
    return call(kernel, out, [SCALARS, WHOLE, WHOLE], 10 * rows * packed)(place, mine, other)


def middle(z, place, tok, pieces, turned, blocks, own):
    total, width = tok.shape
    cut, cols = blocks[0][0].shape
    hid = 2 * cut // 3
    unit, tail = N_X * own, width // (own - 1)
    block = N_Y * unit
    flat = [part for _, held in pieces for part in held]
    n, m = len(flat), len(pieces)

    def kernel(z_ref, place_ref, tok_ref, *refs):
        piece_refs, turned_refs, block_refs = refs[:n], refs[n : n + 4], refs[n + 4 : n + 12]
        first_ref, grd_out, hidden_ref, out = refs[n + 12 : n + 16]
        packed = refs[n + 16 : n + 16 + m]
        x, wt, w, grd, g, pre, by_z, held, sems, out_sems = refs[n + 16 + m :]

        def bring(source, target, i):
            copy = pltpu.make_async_copy(source, target, sems.at[i])
            copy.start()
            return copy

        def spot(dz):
            return lax.rem(z_ref[0] + dz, N_Z)

        def at(b):
            return pl.ds(pl.multiple_of(place_ref[b] * cols, cols), cols)

        come_wt, come_x = [], []
        for b in range(4):
            come_wt.append(bring(turned_refs[b], wt.at[b], n + b))
            come_x.append(bring(tok_ref.at[:, at(b)], x.at[b], n + 4 + b))
        come, i = [], 0
        for target, (_, parts) in zip(packed, pieces):
            size = target.shape[1] // len(parts)
            for j in range(len(parts)):
                come.append(bring(piece_refs[i], target.at[:, j * size : (j + 1) * size], i))
                i += 1
        come_w = []
        for b in range(4):
            top, bottom = block_refs[2 * b], block_refs[2 * b + 1].at[: 2 * hid - cut, :]
            come_w.append(bring(top, w.at[b, :cut, :], n + 8 + b))
            come_w.append(bring(bottom, w.at[b, cut:, :], n + 12 + b))
        acc = None
        for b in range(4):
            come_wt[b].wait()
            come_x[b].wait()
            part = jnp.dot(x[b], wt[b, :, : 2 * hid], preferred_element_type=F32)
            acc = part if b == 0 else acc + part
        for i in range(N_Z):
            pre[i] = acc[i * block : (i + 1) * block]
        for copy in come:
            copy.wait()
        for source, (firsts, _) in zip(packed, pieces):
            for i, first in enumerate(firsts):
                value = source[8 * i : 8 * i + 8, :]
                top = first * own
                grd[top : top + own - 1, :] = value[:, :width]
                for j in range(own - 1):
                    part = value[j : j + 1, width:]
                    grd[top + own - 1 : top + own, j * tail : (j + 1) * tail] = part
        gone = [pltpu.make_async_copy(grd, grd_out, sems.at[0])]
        gone[0].start()
        for b in range(4):
            part = jnp.dot(grd[:, at(b)], wt[b, :, 2 * hid :], preferred_element_type=F32)
            acc = part if b == 0 else acc + part
        g[...] = acc
        for dz in range(N_Z):
            gate_pre, up_pre = pre[spot(dz), :, :hid], pre[spot(dz), :, hid:]
            rows = [slice((dy * N_Z + dz) * unit, (dy * N_Z + dz + 1) * unit) for dy in range(N_Y)]
            grad = jnp.concatenate([g[r, :] for r in rows], axis=0)
            sigma = jax.nn.sigmoid(gate_pre)
            swish = gate_pre * sigma
            hidden = (swish * up_pre).astype(BF)
            up_grad = (grad * swish).astype(BF)
            gate_grad = (grad * up_pre * sigma * (1.0 + gate_pre * (1.0 - sigma))).astype(BF)
            both = jnp.concatenate([gate_grad, up_grad], axis=1)
            first_ref[spot(dz)] = both
            by_z[dz * block : (dz + 1) * block, :] = both
            for dy in range(N_Y):
                hidden_ref[rows[dy], :] = hidden[dy * unit : (dy + 1) * unit]
        for b in range(4):
            come_w[2 * b].wait()
            come_w[2 * b + 1].wait()
            part = jnp.dot(by_z[...], w[b], preferred_element_type=F32).astype(BF)
            for dz in range(N_Z):
                held[b, dz] = part[dz * block : (dz + 1) * block]
                there = out.at[spot(dz), :, b * cols : (b + 1) * cols]
                gone.append(pltpu.make_async_copy(held.at[b, dz], there, out_sems.at[b, dz]))
                gone[-1].start()
        for copy in gone:
            copy.wait()

    first, grd, hidden, sums = call(
        kernel,
        [
            jax.ShapeDtypeStruct((N_Z, block, 2 * hid), BF),
            jax.ShapeDtypeStruct((total, width), BF),
            jax.ShapeDtypeStruct((total, hid), BF),
            jax.ShapeDtypeStruct((N_Z, block, width), BF),
        ],
        [SCALARS] * 2 + [ANYWHERE] * (n + 13),
        8 * total * width + 12 * hid * width,
        flops=10 * total * hid * width,
        limit=BIG_LIMIT,
        out_specs=[WHOLE, ANYWHERE, WHOLE, ANYWHERE],
        scratch_shapes=[
            pltpu.VMEM((8 * len(firsts), width + tail), BF) for firsts, _ in pieces
        ]
        + [
            pltpu.VMEM((4, total, cols), BF),
            pltpu.VMEM((4, cols, 3 * hid), BF),
            pltpu.VMEM((4, 2 * hid, cols), BF),
            pltpu.VMEM((total, width), BF),
            pltpu.VMEM((total, hid), F32),
            pltpu.VMEM((N_Z, block, 2 * hid), F32),
            pltpu.VMEM((total, 2 * hid), BF),
            pltpu.VMEM((4, N_Z, block, cols), BF),
            pltpu.SemaphoreType.DMA((n + 16,)),
            pltpu.SemaphoreType.DMA((4, N_Z)),
        ],
    )(z, place, tok, *flat, *turned, *[half for pair in blocks for half in pair])
    return first.reshape(total, 2 * hid), grd, hidden, sums.reshape(total, width)


def weight_grads(order, lefts, rights):
    hid, cols, n = lefts[0].shape[1], rights[0].shape[1] // 4, len(lefts)
    rows = lefts[0].shape[0]

    def kernel(order_ref, *refs):
        give_ref, keep_ref, held, sems = refs[2 * n :]
        come = {}
        for b in range(4):
            where = pl.ds(pl.multiple_of(order_ref[b] * cols, cols), cols)
            for i, right in enumerate(refs[n : 2 * n]):
                there = held.at[b, i * rows : (i + 1) * rows, :]
                come[b, i] = pltpu.make_async_copy(right.at[:, where], there, sems.at[b, i])
                come[b, i].start()
        left = jnp.concatenate([ref[...] for ref in refs[:n]], axis=0).T
        for b in range(4):
            for i in range(n):
                come[b, i].wait()
            part = jnp.dot(left, held[b], preferred_element_type=F32)
            if b < 2:
                give_ref[b] = part.astype(BF)
            else:
                keep_ref[b - 2] = part

    return call(
        kernel,
        [jax.ShapeDtypeStruct((2, hid, cols), BF), jax.ShapeDtypeStruct((2, hid, cols), F32)],
        [SCALARS] + [WHOLE] * n + [ANYWHERE] * n,
        12 * hid * cols + 8 * n * rows * cols,
        flops=8 * n * rows * hid * cols,
        limit=BIG_LIMIT,
        scratch_shapes=[
            pltpu.VMEM((4, n * rows, cols), BF),
            pltpu.SemaphoreType.DMA((4, n)),
        ],
    )(order, *lefts, *rights)


def per_device(tokens, out_grad, gate_weight, up_weight, down_weight, block_mask, assignment):
    own, width = tokens.shape
    hid, cols = gate_weight.shape
    panels, col_blocks = hid // BLK, cols // BLK
    unit = 2 * own
    x_hi, core, z = (lax.axis_index(a) for a in ("x_hi", "core", "z"))
    place = jnp.stack(
        [2 * x_hi + core, 2 * (1 - x_hi) + core, 2 * x_hi + 1 - core, 2 * (1 - x_hi) + 1 - core]
    )
    tie = lax.optimization_barrier

    panel_ids = lax.broadcasted_iota(jnp.int32, (panels, block_mask.shape[1]), 1)
    selector = (assignment[:, None] == panel_ids).astype(F32)
    slot_mask = jnp.einsum("sp,mpb->msb", selector, block_mask.astype(F32))
    slot_mask = lax.dynamic_slice_in_dim(slot_mask, place[0] * col_blocks, col_blocks, 2)
    keep = jnp.repeat(slot_mask, BLK, axis=2)

    mine = pack([tokens, out_grad])
    tok16, grd16 = by_array(mine, fetch(mine, "x_lo", 1))
    kept = mask_weights([gate_weight, up_weight, down_weight], keep.reshape(-1, cols))
    tok16, grd16, kept = tie((tok16, grd16, kept))

    t1, t3, t2 = fetch(tok16, "y", 1), fetch(tok16, "y", -1), fetch(tok16, "y", 2)
    z1, z7 = fetch(grd16, "z", 1), fetch(grd16, "z", -1)
    z1, z7, t1, t3, t2 = tie((z1, z7, t1, t3, t2))
    tok = unpack(
        [([2 * dy, 2 * dy + 1], [t]) for dy, t in enumerate((tok16, t1, t2, t3))], N_X * N_Y, own, width
    )
    tok = lax.all_gather(tok, "z", axis=0, tiled=True)
    away = [fetch(kept[0], "x_hi", 1)]
    beside_kept = [fetch(half, "core", 1) for half in kept]
    z2, z6, beside_kept = tie((fetch(z1, "z", 1), fetch(z7, "z", -1), beside_kept))
    near = stack([grd16, z1, z7, z2, z6])
    cut = near.shape[1] // 2
    n1, n3 = fetch(near, "y", 1), fetch(near, "y", -1)
    z3, z5 = tie((fetch(z2, "z", 1), fetch(z6, "z", -1)))
    z4 = [fetch(z3[:, :cut], "z", 1), fetch(z5[:, cut:], "z", -1)]
    z4, later = tie((z4, kept[1]))
    rest = join([[z3], [z5], z4])
    kept_turned = turn(kept)
    n1, n3, rest, kept_turned, away = tie((n1, n3, rest, kept_turned, away))
    n2 = [fetch(n1[:, :cut], "y", 1), fetch(n3[:, cut:], "y", -1)]
    r1, r3 = fetch(rest, "y", 1), fetch(rest, "y", -1)
    away = [away[0], fetch(later, "x_hi", 1)]
    n2, r1, r3, away = tie((n2, r1, r3, away))
    r2 = [fetch(r1[:, :cut], "y", 1), fetch(r3[:, cut:], "y", -1)]
    beside_away = [fetch(half, "core", 1) for half in away]
    blocks = [kept, away, beside_kept, beside_away]
    turned = [kept_turned, turn(away), turn(beside_kept), turn(beside_away)]
    tok, r2, turned = tie((tok, r2, turned))
    pieces = []
    for dy, n, r in ((0, [near], [rest]), (1, [n1], [r1]), (2, n2, r2), (3, [n3], [r3])):
        for offsets, held in (((0, 1, 7, 2, 6), n), ((3, 5, 4), r)):
            pieces.append(([2 * (N_Z * dy + dz) + dx for dz in offsets for dx in range(N_X)], held))
    by_z, grd, hidden, total = middle(z[None], place, tok, pieces, turned, blocks, own)
    total = lax.psum_scatter(total, "z", scatter_dimension=0, tiled=True)

    order = place[::-1]
    give_a, keep_a = weight_grads(order, [by_z], [tok])
    give_a = fetch(give_a, "core", 1)
    give_b, keep_b = weight_grads(order, [hidden], [grd])
    give_a, give_b, keep_b = tie((give_a, give_b, keep_b))
    far_a = fetch((keep_a[0] + give_a[0].astype(F32)).astype(BF), "x_hi", 1)
    give_b = fetch(give_b, "core", 1)
    far_b = fetch((keep_b[0] + give_b[0].astype(F32)).astype(BF), "x_hi", 1)

    def finish(keep_sum, give, far, rows):
        total = keep_sum[1] + give[1].astype(F32) + far.astype(F32)
        total = total.reshape(-1, panels, BLK, cols) * rows[:, :, None, :]
        return total.astype(BF).reshape(-1, hid, cols)

    gate_up_grad = finish(keep_a, give_a, far_a, keep[:2])
    down_grad = finish(keep_b, give_b, far_b, keep[2:])

    parts = deal(total, own)
    parts = [parts[0]] + [fetch(parts[dy], "y", -dy) for dy in (1, 3, 2)]

    def last(*parts):
        both = sum(part.astype(F32) for part in parts)
        return both[: own - 1], both[own - 1 :]

    parts, gate_up_grad, down_grad = tie((parts, gate_up_grad, down_grad))
    mine, other = local(last, *parts)
    input_grad = place_rows(place, mine, fetch(other, "x_lo", 1))
    return (input_grad, gate_up_grad[0], gate_up_grad[1], down_grad[0])


def solution(mesh):
    fine = Mesh(mesh.devices.reshape(SIZES), AXES)
    rows = P(DP + MP, None)
    weights = P(MP, DP)
    return jax.shard_map(
        per_device,
        mesh=fine,
        in_specs=(rows, rows, weights, weights, weights, P(), P(MP)),
        out_specs=(rows, weights, weights, weights),
        check_vma=False,
    )
```

```python
import jax
import jax.numpy as jnp
from jax import lax
from jax.experimental import pallas as pl
from jax.experimental.pallas import tpu as pltpu
from jax.sharding import Mesh
from jax.sharding import PartitionSpec as P

BLK = 128
AXES = ("x_hi", "core", "x_lo", "y", "z")
SIZES = (2, 2, 2, 4, 8)
DP = ("x_hi", "core")
MP = ("x_lo", "y", "z")
N_X, N_Y, N_Z = 2, 4, 8
BF = jnp.bfloat16
F32 = jnp.float32
WHOLE = pl.BlockSpec(memory_space=pltpu.VMEM)
VMEM_LIMIT = 6 << 20
BIG_LIMIT = 52 << 20
ANYWHERE = pl.BlockSpec(memory_space=pl.ANY)
SCALARS = pl.BlockSpec(memory_space=pltpu.SMEM)


def call(kernel, out_shape, in_specs, bytes_accessed, flops=0, **more):
    return pl.pallas_call(
        kernel,
        out_shape=out_shape,
        in_specs=in_specs,
        out_specs=more.pop("out_specs", jax.tree.map(lambda _: WHOLE, out_shape)),
        compiler_params=pltpu.CompilerParams(vmem_limit_bytes=more.pop("limit", VMEM_LIMIT)),
        cost_estimate=pl.CostEstimate(
            flops=flops, bytes_accessed=bytes_accessed, transcendentals=0
        ),
        **more,
    )


def local(function, *arrays):
    out = jax.eval_shape(function, *arrays)

    def kernel(*refs):
        results = function(*(ref[...] for ref in refs[: len(arrays)]))
        for ref, value in zip(refs[len(arrays) :], results):
            ref[...] = value

    size = sum(a.size * a.dtype.itemsize for a in (*arrays, *out))
    return call(kernel, list(out), [WHOLE] * len(arrays), size)(*arrays)


def fetch(block, axis, offset):
    size = SIZES[AXES.index(axis)]
    return lax.ppermute(block, axis, [(i, (i - offset) % size) for i in range(size)])


def pack(arrays):
    own, width = arrays[0].shape
    tail, rows = width // (own - 1), own - 1

    def kernel(*refs):
        out = refs[-1]
        for k, ref in enumerate(refs[:-1]):
            out[k * rows : (k + 1) * rows, :width] = ref[:rows, :]
            for i in range(rows):
                spot = k * rows + i
                out[spot : spot + 1, width:] = ref[rows : rows + 1, i * tail : (i + 1) * tail]

    out = jax.ShapeDtypeStruct((rows * len(arrays), width + tail), BF)
    return call(kernel, out, [WHOLE] * len(arrays), 4 * own * width * len(arrays))(*arrays)


def by_array(mine, other):
    rows = mine.shape[0] // 2

    def kernel(mine_ref, other_ref, *out):
        for k in range(2):
            out[k][:rows, :] = mine_ref[k * rows : (k + 1) * rows, :]
            out[k][rows:, :] = other_ref[k * rows : (k + 1) * rows, :]

    out = [jax.ShapeDtypeStruct(mine.shape, BF)] * 2
    return call(kernel, out, [WHOLE] * 2, 4 * mine.shape[0] * mine.shape[1])(mine, other)


def stack(blocks):
    starts = [sum(b.shape[0] for b in blocks[:i]) for i in range(len(blocks) + 1)]

    def kernel(*refs):
        for ref, start in zip(refs[:-1], starts):
            refs[-1][start : start + ref.shape[0], :] = ref[...]

    whole = jax.ShapeDtypeStruct((starts[-1], blocks[0].shape[1]), blocks[0].dtype)
    size = 4 * starts[-1] * blocks[0].shape[1]
    return call(kernel, whole, [WHOLE] * len(blocks), size)(*blocks)


def join(lines):
    spots, flat, top = [], [], 0
    for line in lines:
        left = 0
        for block in line:
            spots.append((top, left))
            flat.append(block)
            left += block.shape[1]
        top += line[0].shape[0]

    def kernel(*refs):
        for ref, (row, col) in zip(refs[:-1], spots):
            refs[-1][row : row + ref.shape[0], col : col + ref.shape[1]] = ref[...]

    whole = jax.ShapeDtypeStruct((top, left), flat[0].dtype)
    return call(kernel, whole, [WHOLE] * len(flat), 4 * top * left)(*flat)


def unpack(pieces, units, own, width):
    tail = width // (own - 1)
    flat = [block for _, blocks in pieces for block in blocks]

    def kernel(*refs):
        out, at = refs[-1], 0
        for firsts, blocks in pieces:
            held = refs[at : at + len(blocks)]
            at += len(blocks)
            for i, unit in enumerate(firsts):
                rows = slice(8 * i, 8 * i + 8)
                top = unit * own
                value = jnp.concatenate([ref[rows, :] for ref in held], axis=1)
                out[top : top + own - 1, :] = value[:, :width]
                for j in range(own - 1):
                    part = value[j : j + 1, width:]
                    out[top + own - 1 : top + own, j * tail : (j + 1) * tail] = part

    whole = jax.ShapeDtypeStruct((units * own, width), BF)
    return call(kernel, whole, [WHOLE] * len(flat), 4 * units * own * width)(*flat)


def mask_weights(weights, keep_rows):
    rows, cols = weights[0].shape
    panels = rows // BLK

    def kernel(keep_ref, *refs):
        for m in range(len(weights)):
            for p in range(panels):
                row = m * panels + p
                keep = keep_ref[row : row + 1, :]
                kept = refs[m][p * BLK : (p + 1) * BLK, :].astype(F32) * keep
                half, row = divmod(row, len(weights) * panels // 2)
                refs[half - 2][row * BLK : (row + 1) * BLK, :] = kept.astype(BF)

    out = [jax.ShapeDtypeStruct((rows * len(weights) // 2, cols), BF)] * 2
    return call(kernel, out, [WHOLE] * 4, 12 * rows * cols)(keep_rows, *weights)


def turn(halves):
    rows, cols = halves[0].shape

    def kernel(top, bottom, out):
        out[:, :rows] = top[...].T
        out[:, rows:] = bottom[...].T

    out = jax.ShapeDtypeStruct((cols, 2 * rows), BF)
    return call(kernel, out, [WHOLE] * 2, 8 * rows * cols)(*halves)


def deal(total, own):
    width = total.shape[1]
    unit, rows, tail = N_X * own, own - 1, width // (own - 1)
    count = total.shape[0] // unit

    def kernel(ref, *out):
        for u in range(count):
            for k in range(N_X):
                top = u * unit + k * own
                out[u][k * rows : (k + 1) * rows, :width] = ref[top : top + rows, :]
                for i in range(rows):
                    part = ref[top + rows : top + own, i * tail : (i + 1) * tail]
                    out[u][k * rows + i : k * rows + i + 1, width:] = part

    spec = [jax.ShapeDtypeStruct((N_X * rows, width + tail), BF)] * count
    return call(kernel, spec, [WHOLE], 6 * total.shape[0] * width)(total)


def place_rows(place, mine, other):
    rows, packed = mine.shape
    width = packed * rows // (rows + 1)
    cols, tail = width // 4, width // rows

    def kernel(place_ref, mine_ref, other_ref, out):
        total = (mine_ref[...] + other_ref[...]).astype(BF)
        for b in range(4):
            start = place_ref[b] * cols
            where = pl.ds(pl.multiple_of(start, tail), cols)
            out[:rows, where] = total[:, b * cols : (b + 1) * cols]
            for j in range(cols // tail):
                i = b * (cols // tail) + j
                where = pl.ds(pl.multiple_of(start + j * tail, tail), tail)
                out[rows : rows + 1, where] = total[i : i + 1, width:]

    out = jax.ShapeDtypeStruct((rows + 1, width), BF)
    return call(kernel, out, [SCALARS, WHOLE, WHOLE], 10 * rows * packed)(place, mine, other)


def middle(z, place, tok, pieces, turned, blocks, own):
    total, width = tok.shape
    cut, cols = blocks[0][0].shape
    hid = 2 * cut // 3
    unit, tail = N_X * own, width // (own - 1)
    block = N_Y * unit
    flat = [part for _, held in pieces for part in held]
    n, m = len(flat), len(pieces)

    def kernel(z_ref, place_ref, tok_ref, *refs):
        piece_refs, turned_refs, block_refs = refs[:n], refs[n : n + 4], refs[n + 4 : n + 12]
        first_ref, grd_out, hidden_ref, out = refs[n + 12 : n + 16]
        packed = refs[n + 16 : n + 16 + m]
        x, wt, w, grd, g, total_ref, pre, by_z, held, sems, out_sems = refs[n + 16 + m :]

        def bring(source, target, i):
            copy = pltpu.make_async_copy(source, target, sems.at[i])
            copy.start()
            return copy

        def spot(dz):
            return lax.rem(z_ref[0] + dz, N_Z)

        def at(b):
            return pl.ds(pl.multiple_of(place_ref[b] * cols, cols), cols)

        for b in range(4):
            bring(turned_refs[b], wt.at[b], n + b)
            bring(tok_ref.at[:, at(b)], x.at[b], n + 4 + b)
        come, i = [], 0
        for target, (_, parts) in zip(packed, pieces):
            size = target.shape[1] // len(parts)
            for j in range(len(parts)):
                come.append(bring(piece_refs[i], target.at[:, j * size : (j + 1) * size], i))
                i += 1
        come_w = []
        for b in range(4):
            top, bottom = block_refs[2 * b], block_refs[2 * b + 1].at[: 2 * hid - cut, :]
            come_w.append(bring(top, w.at[b, :cut, :], n + 8 + b))
            come_w.append(bring(bottom, w.at[b, cut:, :], n + 12 + b))
        def pre_part(b, _):
            pltpu.make_async_copy(turned_refs[0], wt.at[b], sems.at[n + b]).wait()
            pltpu.make_async_copy(tok_ref.at[:, :cols], x.at[b], sems.at[n + 4 + b]).wait()
            part = jnp.dot(x[b], wt[b, :, : 2 * hid], preferred_element_type=F32)

            @pl.when(b == 0)
            def _():
                total_ref[...] = part

            @pl.when(b > 0)
            def _():
                total_ref[...] += part

            return 0

        lax.fori_loop(0, 4, pre_part, 0)
        for i in range(N_Z):
            pre[i] = total_ref[i * block : (i + 1) * block, :]
        for copy in come:
            copy.wait()
        for source, (firsts, _) in zip(packed, pieces):
            for i, first in enumerate(firsts):
                value = source[8 * i : 8 * i + 8, width:]
                top = first * own
                for j in range(own - 1):
                    spot_j = slice(j * tail, (j + 1) * tail)
                    grd[top + own - 1 : top + own, spot_j] = value[j : j + 1]

        def columns(c, _):
            where = pl.ds(pl.multiple_of(c * tail, tail), tail)
            for source, (firsts, _) in zip(packed, pieces):
                for i, first in enumerate(firsts):
                    top = first * own
                    grd[top : top + own - 1, where] = source[8 * i : 8 * i + 8, where]
            return 0

        lax.fori_loop(0, own - 1, columns, 0)
        gone = [pltpu.make_async_copy(grd, grd_out, sems.at[0])]
        gone[0].start()
        g[...] = jnp.zeros_like(g)

        def grad_part(b, _):
            g[...] += jnp.dot(grd[:, at(b)], wt[b, :, 2 * hid :], preferred_element_type=F32)
            return 0

        lax.fori_loop(0, 4, grad_part, 0)
        for dz in range(N_Z):
            gate_pre, up_pre = pre[spot(dz), :, :hid], pre[spot(dz), :, hid:]
            rows = [slice((dy * N_Z + dz) * unit, (dy * N_Z + dz + 1) * unit) for dy in range(N_Y)]
            grad = jnp.concatenate([g[r, :] for r in rows], axis=0)
            sigma = jax.nn.sigmoid(gate_pre)
            swish = gate_pre * sigma
            hidden = (swish * up_pre).astype(BF)
            up_grad = (grad * swish).astype(BF)
            gate_grad = (grad * up_pre * sigma * (1.0 + gate_pre * (1.0 - sigma))).astype(BF)
            both = jnp.concatenate([gate_grad, up_grad], axis=1)
            first_ref[spot(dz)] = both
            by_z[dz * block : (dz + 1) * block, :] = both
            for dy in range(N_Y):
                hidden_ref[rows[dy], :] = hidden[dy * unit : (dy + 1) * unit]
        for copy in come_w:
            copy.wait()

        def send(b, dz):
            there = out.at[spot(dz), :, pl.ds(pl.multiple_of(b * cols, cols), cols)]
            return pltpu.make_async_copy(held.at[b, dz], there, out_sems.at[b, dz])

        def spread_part(b, _):
            part = jnp.dot(by_z[...], w[b], preferred_element_type=F32).astype(BF)
            for dz in range(N_Z):
                held[b, dz] = part[dz * block : (dz + 1) * block]
                send(b, dz).start()
            return 0

        lax.fori_loop(0, 4, spread_part, 0)

        def sent(i, _):
            send(i // N_Z, i % N_Z).wait()
            return 0

        lax.fori_loop(0, 4 * N_Z, sent, 0)
        for copy in gone:
            copy.wait()

    first, grd, hidden, sums = call(
        kernel,
        [
            jax.ShapeDtypeStruct((N_Z, block, 2 * hid), BF),
            jax.ShapeDtypeStruct((total, width), BF),
            jax.ShapeDtypeStruct((total, hid), BF),
            jax.ShapeDtypeStruct((N_Z, block, width), BF),
        ],
        [SCALARS] * 2 + [ANYWHERE] * (n + 13),
        8 * total * width + 12 * hid * width,
        flops=10 * total * hid * width,
        limit=BIG_LIMIT,
        out_specs=[WHOLE, ANYWHERE, WHOLE, ANYWHERE],
        scratch_shapes=[
            pltpu.VMEM((8 * len(firsts), width + tail), BF) for firsts, _ in pieces
        ]
        + [
            pltpu.VMEM((4, total, cols), BF),
            pltpu.VMEM((4, cols, 3 * hid), BF),
            pltpu.VMEM((4, 2 * hid, cols), BF),
            pltpu.VMEM((total, width), BF),
            pltpu.VMEM((total, hid), F32),
            pltpu.VMEM((total, 2 * hid), F32),
            pltpu.VMEM((N_Z, block, 2 * hid), F32),
            pltpu.VMEM((total, 2 * hid), BF),
            pltpu.VMEM((4, N_Z, block, cols), BF),
            pltpu.SemaphoreType.DMA((n + 16,)),
            pltpu.SemaphoreType.DMA((4, N_Z)),
        ],
    )(z, place, tok, *flat, *turned, *[half for pair in blocks for half in pair])
    return first.reshape(total, 2 * hid), grd, hidden, sums.reshape(total, width)


def weight_grads(order, lefts, rights):
    hid, cols, n = lefts[0].shape[1], rights[0].shape[1] // 4, len(lefts)
    rows = lefts[0].shape[0]

    def kernel(order_ref, *refs):
        give_ref, keep_ref, held, turned_ref, sems = refs[2 * n :]
        for b in range(4):
            where = pl.ds(pl.multiple_of(order_ref[b] * cols, cols), cols)
            for i, right in enumerate(refs[n : 2 * n]):
                there = held.at[b, i * rows : (i + 1) * rows, :]
                pltpu.make_async_copy(right.at[:, where], there, sems.at[b, i]).start()
        left = jnp.concatenate([ref[...] for ref in refs[:n]], axis=0).T
        turned_ref[...] = left

        def column_part(b, _):
            for i, right in enumerate(refs[n : 2 * n]):
                there = held.at[b, i * rows : (i + 1) * rows, :]
                pltpu.make_async_copy(right.at[:, :cols], there, sems.at[b, i]).wait()
            part = jnp.dot(turned_ref[...], held[b], preferred_element_type=F32)

            @pl.when(b < 2)
            def _():
                give_ref[b] = part.astype(BF)

            @pl.when(b >= 2)
            def _():
                keep_ref[b - 2] = part

            return 0

        lax.fori_loop(0, 4, column_part, 0)

    return call(
        kernel,
        [jax.ShapeDtypeStruct((2, hid, cols), BF), jax.ShapeDtypeStruct((2, hid, cols), F32)],
        [SCALARS] + [WHOLE] * n + [ANYWHERE] * n,
        12 * hid * cols + 8 * n * rows * cols,
        flops=8 * n * rows * hid * cols,
        limit=BIG_LIMIT,
        scratch_shapes=[
            pltpu.VMEM((4, n * rows, cols), BF),
            pltpu.VMEM((hid, n * rows), BF),
            pltpu.SemaphoreType.DMA((4, n)),
        ],
    )(order, *lefts, *rights)


def per_device(tokens, out_grad, gate_weight, up_weight, down_weight, block_mask, assignment):
    own, width = tokens.shape
    hid, cols = gate_weight.shape
    panels, col_blocks = hid // BLK, cols // BLK
    unit = 2 * own
    x_hi, core, z = (lax.axis_index(a) for a in ("x_hi", "core", "z"))
    place = jnp.stack(
        [2 * x_hi + core, 2 * (1 - x_hi) + core, 2 * x_hi + 1 - core, 2 * (1 - x_hi) + 1 - core]
    )
    tie = lax.optimization_barrier

    panel_ids = lax.broadcasted_iota(jnp.int32, (panels, block_mask.shape[1]), 1)
    selector = (assignment[:, None] == panel_ids).astype(F32)
    slot_mask = jnp.einsum("sp,mpb->msb", selector, block_mask.astype(F32))
    slot_mask = lax.dynamic_slice_in_dim(slot_mask, place[0] * col_blocks, col_blocks, 2)
    keep = jnp.repeat(slot_mask, BLK, axis=2)

    mine = pack([tokens, out_grad])
    tok16, grd16 = by_array(mine, fetch(mine, "x_lo", 1))
    kept = mask_weights([gate_weight, up_weight, down_weight], keep.reshape(-1, cols))
    tok16, grd16, kept = tie((tok16, grd16, kept))

    t1, t3, t2 = fetch(tok16, "y", 1), fetch(tok16, "y", -1), fetch(tok16, "y", 2)
    z1, z7 = fetch(grd16, "z", 1), fetch(grd16, "z", -1)
    z1, z7, t1, t3, t2 = tie((z1, z7, t1, t3, t2))
    tok = unpack(
        [([2 * dy, 2 * dy + 1], [t]) for dy, t in enumerate((tok16, t1, t2, t3))], N_X * N_Y, own, width
    )
    tok = lax.all_gather(tok, "z", axis=0, tiled=True)
    away = [fetch(kept[0], "x_hi", 1)]
    beside_kept = [fetch(half, "core", 1) for half in kept]
    z2, z6, beside_kept = tie((fetch(z1, "z", 1), fetch(z7, "z", -1), beside_kept))
    near = stack([grd16, z1, z7, z2, z6])
    cut = near.shape[1] // 2
    n1, n3 = fetch(near, "y", 1), fetch(near, "y", -1)
    z3, z5 = tie((fetch(z2, "z", 1), fetch(z6, "z", -1)))
    z4 = [fetch(z3[:, :cut], "z", 1), fetch(z5[:, cut:], "z", -1)]
    z4, later = tie((z4, kept[1]))
    rest = join([[z3], [z5], z4])
    kept_turned = turn(kept)
    n1, n3, rest, kept_turned, away = tie((n1, n3, rest, kept_turned, away))
    n2 = [fetch(n1[:, :cut], "y", 1), fetch(n3[:, cut:], "y", -1)]
    r1, r3 = fetch(rest, "y", 1), fetch(rest, "y", -1)
    away = [away[0], fetch(later, "x_hi", 1)]
    n2, r1, r3, away = tie((n2, r1, r3, away))
    r2 = [fetch(r1[:, :cut], "y", 1), fetch(r3[:, cut:], "y", -1)]
    beside_away = [fetch(half, "core", 1) for half in away]
    blocks = [kept, away, beside_kept, beside_away]
    turned = [kept_turned, turn(away), turn(beside_kept), turn(beside_away)]
    tok, r2, turned = tie((tok, r2, turned))
    pieces = []
    for dy, n, r in ((0, [near], [rest]), (1, [n1], [r1]), (2, n2, r2), (3, [n3], [r3])):
        for offsets, held in (((0, 1, 7, 2, 6), n), ((3, 5, 4), r)):
            pieces.append(([2 * (N_Z * dy + dz) + dx for dz in offsets for dx in range(N_X)], held))
    by_z, grd, hidden, total = middle(z[None], place, tok, pieces, turned, blocks, own)
    total = lax.psum_scatter(total, "z", scatter_dimension=0, tiled=True)

    order = place[::-1]
    give_a, keep_a = weight_grads(order, [by_z], [tok])
    give_a = fetch(give_a, "core", 1)
    give_b, keep_b = weight_grads(order, [hidden], [grd])
    give_a, give_b, keep_b = tie((give_a, give_b, keep_b))
    far_a = fetch((keep_a[0] + give_a[0].astype(F32)).astype(BF), "x_hi", 1)
    give_b = fetch(give_b, "core", 1)
    far_b = fetch((keep_b[0] + give_b[0].astype(F32)).astype(BF), "x_hi", 1)

    def finish(keep_sum, give, far, rows):
        total = keep_sum[1] + give[1].astype(F32) + far.astype(F32)
        total = total.reshape(-1, panels, BLK, cols) * rows[:, :, None, :]
        return total.astype(BF).reshape(-1, hid, cols)

    gate_up_grad = finish(keep_a, give_a, far_a, keep[:2])
    down_grad = finish(keep_b, give_b, far_b, keep[2:])

    parts = deal(total, own)
    parts = [parts[0]] + [fetch(parts[dy], "y", -dy) for dy in (1, 3, 2)]

    def last(*parts):
        both = sum(part.astype(F32) for part in parts)
        return both[: own - 1], both[own - 1 :]

    parts, gate_up_grad, down_grad = tie((parts, gate_up_grad, down_grad))
    mine, other = local(last, *parts)
    input_grad = place_rows(place, mine, fetch(other, "x_lo", 1))
    return (input_grad, gate_up_grad[0], gate_up_grad[1], down_grad[0])


def solution(mesh):
    fine = Mesh(mesh.devices.reshape(SIZES), AXES)
    rows = P(DP + MP, None)
    weights = P(MP, DP)
    return jax.shard_map(
        per_device,
        mesh=fine,
        in_specs=(rows, rows, weights, weights, weights, P(), P(MP)),
        out_specs=(rows, weights, weights, weights),
        check_vma=False,
    )
```

```python
import jax
import jax.numpy as jnp
from jax import lax
from jax.experimental import pallas as pl
from jax.experimental.pallas import tpu as pltpu
from jax.sharding import Mesh
from jax.sharding import PartitionSpec as P

BLK = 128
AXES = ("x_hi", "core", "x_lo", "y", "z")
SIZES = (2, 2, 2, 4, 8)
DP = ("x_hi", "core")
MP = ("x_lo", "y", "z")
N_X, N_Y, N_Z = 2, 4, 8
BF = jnp.bfloat16
F32 = jnp.float32
WHOLE = pl.BlockSpec(memory_space=pltpu.VMEM)
VMEM_LIMIT = 6 << 20
BIG_LIMIT = 52 << 20
ANYWHERE = pl.BlockSpec(memory_space=pl.ANY)
SCALARS = pl.BlockSpec(memory_space=pltpu.SMEM)


def call(kernel, out_shape, in_specs, bytes_accessed, flops=0, **more):
    return pl.pallas_call(
        kernel,
        out_shape=out_shape,
        in_specs=in_specs,
        out_specs=more.pop("out_specs", jax.tree.map(lambda _: WHOLE, out_shape)),
        compiler_params=pltpu.CompilerParams(vmem_limit_bytes=more.pop("limit", VMEM_LIMIT)),
        cost_estimate=pl.CostEstimate(
            flops=flops, bytes_accessed=bytes_accessed, transcendentals=0
        ),
        **more,
    )


def local(function, *arrays):
    out = jax.eval_shape(function, *arrays)

    def kernel(*refs):
        results = function(*(ref[...] for ref in refs[: len(arrays)]))
        for ref, value in zip(refs[len(arrays) :], results):
            ref[...] = value

    size = sum(a.size * a.dtype.itemsize for a in (*arrays, *out))
    return call(kernel, list(out), [WHOLE] * len(arrays), size)(*arrays)


def fetch(block, axis, offset):
    size = SIZES[AXES.index(axis)]
    return lax.ppermute(block, axis, [(i, (i - offset) % size) for i in range(size)])


def pack(arrays):
    own, width = arrays[0].shape
    tail, rows, n = width // (own - 1), own - 1, len(arrays)

    def kernel(*refs):
        out, held, sems = refs[n:]
        come = [pltpu.make_async_copy(refs[k], held.at[k], sems.at[k]) for k in range(n)]
        for copy in come:
            copy.start()
        for k in range(n):
            come[k].wait()
            out[k * rows : (k + 1) * rows, :width] = held[k, :rows, :]
            for i in range(rows):
                spot = k * rows + i
                part = held[k, rows : rows + 1, i * tail : (i + 1) * tail]
                out[spot : spot + 1, width:] = part

    return call(
        kernel,
        jax.ShapeDtypeStruct((rows * n, width + tail), BF),
        [ANYWHERE] * n,
        4 * own * width * n,
        limit=BIG_LIMIT,
        scratch_shapes=[pltpu.VMEM((n, own, width), BF), pltpu.SemaphoreType.DMA((n,))],
    )(*arrays)


def by_array(mine, other):
    rows = mine.shape[0] // 2

    def kernel(mine_ref, other_ref, *out):
        for k in range(2):
            out[k][:rows, :] = mine_ref[k * rows : (k + 1) * rows, :]
            out[k][rows:, :] = other_ref[k * rows : (k + 1) * rows, :]

    out = [jax.ShapeDtypeStruct(mine.shape, BF)] * 2
    return call(kernel, out, [WHOLE] * 2, 4 * mine.shape[0] * mine.shape[1])(mine, other)


def stack(blocks):
    starts = [sum(b.shape[0] for b in blocks[:i]) for i in range(len(blocks) + 1)]

    def kernel(*refs):
        for ref, start in zip(refs[:-1], starts):
            refs[-1][start : start + ref.shape[0], :] = ref[...]

    whole = jax.ShapeDtypeStruct((starts[-1], blocks[0].shape[1]), blocks[0].dtype)
    size = 4 * starts[-1] * blocks[0].shape[1]
    return call(kernel, whole, [WHOLE] * len(blocks), size)(*blocks)


def join(lines):
    spots, flat, top = [], [], 0
    for line in lines:
        left = 0
        for block in line:
            spots.append((top, left))
            flat.append(block)
            left += block.shape[1]
        top += line[0].shape[0]

    def kernel(*refs):
        for ref, (row, col) in zip(refs[:-1], spots):
            refs[-1][row : row + ref.shape[0], col : col + ref.shape[1]] = ref[...]

    whole = jax.ShapeDtypeStruct((top, left), flat[0].dtype)
    return call(kernel, whole, [WHOLE] * len(flat), 4 * top * left)(*flat)


def unpack(pieces, units, own, width):
    tail = width // (own - 1)
    flat = [block for _, blocks in pieces for block in blocks]

    def kernel(*refs):
        out, at = refs[-1], 0
        for firsts, blocks in pieces:
            held = refs[at : at + len(blocks)]
            at += len(blocks)
            for i, unit in enumerate(firsts):
                rows = slice(8 * i, 8 * i + 8)
                top = unit * own
                value = jnp.concatenate([ref[rows, :] for ref in held], axis=1)
                out[top : top + own - 1, :] = value[:, :width]
                for j in range(own - 1):
                    part = value[j : j + 1, width:]
                    out[top + own - 1 : top + own, j * tail : (j + 1) * tail] = part

    whole = jax.ShapeDtypeStruct((units * own, width), BF)
    return call(kernel, whole, [WHOLE] * len(flat), 4 * units * own * width)(*flat)


def mask_weights(weights, keep_rows):
    rows, cols = weights[0].shape
    panels = rows // BLK

    def kernel(keep_ref, *refs):
        for m in range(len(weights)):
            for p in range(panels):
                row = m * panels + p
                keep = keep_ref[row : row + 1, :]
                kept = refs[m][p * BLK : (p + 1) * BLK, :].astype(F32) * keep
                half, row = divmod(row, len(weights) * panels // 2)
                refs[half - 2][row * BLK : (row + 1) * BLK, :] = kept.astype(BF)

    out = [jax.ShapeDtypeStruct((rows * len(weights) // 2, cols), BF)] * 2
    return call(kernel, out, [WHOLE] * 4, 12 * rows * cols)(keep_rows, *weights)


def turn(halves):
    rows, cols = halves[0].shape

    def kernel(top, bottom, out, held, turned, sems):
        come = [
            pltpu.make_async_copy(half, held.at[i], sems.at[i])
            for i, half in enumerate((top, bottom))
        ]
        for copy in come:
            copy.start()
        for i in range(2):
            come[i].wait()
            turned[:, i * rows : (i + 1) * rows] = held[i].T
        gone = pltpu.make_async_copy(turned, out, sems.at[2])
        gone.start()
        gone.wait()

    return call(
        kernel,
        jax.ShapeDtypeStruct((cols, 2 * rows), BF),
        [ANYWHERE] * 2,
        8 * rows * cols,
        limit=BIG_LIMIT,
        out_specs=ANYWHERE,
        scratch_shapes=[
            pltpu.VMEM((2, rows, cols), BF),
            pltpu.VMEM((cols, 2 * rows), BF),
            pltpu.SemaphoreType.DMA((3,)),
        ],
    )(*halves)


def deal(total, own):
    width = total.shape[1]
    unit, rows, tail = N_X * own, own - 1, width // (own - 1)
    count = total.shape[0] // unit

    def kernel(ref, *out):
        for u in range(count):
            for k in range(N_X):
                top = u * unit + k * own
                out[u][k * rows : (k + 1) * rows, :width] = ref[top : top + rows, :]
                for i in range(rows):
                    part = ref[top + rows : top + own, i * tail : (i + 1) * tail]
                    out[u][k * rows + i : k * rows + i + 1, width:] = part

    spec = [jax.ShapeDtypeStruct((N_X * rows, width + tail), BF)] * count
    return call(kernel, spec, [WHOLE], 6 * total.shape[0] * width)(total)


def place_rows(place, mine, other):
    rows, packed = mine.shape
    width = packed * rows // (rows + 1)
    cols, tail = width // 4, width // rows

    def kernel(place_ref, mine_ref, other_ref, out):
        total = (mine_ref[...] + other_ref[...]).astype(BF)
        for b in range(4):
            start = place_ref[b] * cols
            where = pl.ds(pl.multiple_of(start, tail), cols)
            out[:rows, where] = total[:, b * cols : (b + 1) * cols]
            for j in range(cols // tail):
                i = b * (cols // tail) + j
                where = pl.ds(pl.multiple_of(start + j * tail, tail), tail)
                out[rows : rows + 1, where] = total[i : i + 1, width:]

    out = jax.ShapeDtypeStruct((rows + 1, width), BF)
    return call(kernel, out, [SCALARS, WHOLE, WHOLE], 10 * rows * packed)(place, mine, other)


def middle(z, place, tok, pieces, turned, blocks, own):
    total, width = tok.shape
    cut, cols = blocks[0][0].shape
    hid = 2 * cut // 3
    unit, tail = N_X * own, width // (own - 1)
    block = N_Y * unit
    flat = [part for _, held in pieces for part in held]
    n, m = len(flat), len(pieces)

    def kernel(z_ref, place_ref, tok_ref, *refs):
        piece_refs, turned_refs, block_refs = refs[:n], refs[n : n + 4], refs[n + 4 : n + 12]
        first_out, grd_out, hidden_out, out = refs[n + 12 : n + 16]
        packed = refs[n + 16 : n + 16 + m]
        x, wt, w, grd, g, total_ref, pre, by_z, first_ref, hidden_ref, held, sems, out_sems = refs[n + 16 + m :]

        def bring(source, target, i):
            copy = pltpu.make_async_copy(source, target, sems.at[i])
            copy.start()
            return copy

        def spot(dz):
            return lax.rem(z_ref[0] + dz, N_Z)

        def at(b):
            return pl.ds(pl.multiple_of(place_ref[b] * cols, cols), cols)

        for b in range(4):
            bring(turned_refs[b], wt.at[b], n + b)
            bring(tok_ref.at[:, at(b)], x.at[b], n + 4 + b)
        come, i = [], 0
        for target, (_, parts) in zip(packed, pieces):
            size = target.shape[1] // len(parts)
            for j in range(len(parts)):
                come.append(bring(piece_refs[i], target.at[:, j * size : (j + 1) * size], i))
                i += 1
        come_w = []
        for b in range(4):
            top, bottom = block_refs[2 * b], block_refs[2 * b + 1].at[: 2 * hid - cut, :]
            come_w.append(bring(top, w.at[b, :cut, :], n + 8 + b))
            come_w.append(bring(bottom, w.at[b, cut:, :], n + 12 + b))
        def pre_part(b, _):
            pltpu.make_async_copy(turned_refs[0], wt.at[b], sems.at[n + b]).wait()
            pltpu.make_async_copy(tok_ref.at[:, :cols], x.at[b], sems.at[n + 4 + b]).wait()
            part = jnp.dot(x[b], wt[b, :, : 2 * hid], preferred_element_type=F32)

            @pl.when(b == 0)
            def _():
                total_ref[...] = part

            @pl.when(b > 0)
            def _():
                total_ref[...] += part

            return 0

        lax.fori_loop(0, 4, pre_part, 0)
        for i in range(N_Z):
            pre[i] = total_ref[i * block : (i + 1) * block, :]
        for copy in come:
            copy.wait()
        for source, (firsts, _) in zip(packed, pieces):
            for i, first in enumerate(firsts):
                value = source[8 * i : 8 * i + 8, width:]
                top = first * own
                for j in range(own - 1):
                    spot_j = slice(j * tail, (j + 1) * tail)
                    grd[top + own - 1 : top + own, spot_j] = value[j : j + 1]

        def columns(c, _):
            where = pl.ds(pl.multiple_of(c * tail, tail), tail)
            for source, (firsts, _) in zip(packed, pieces):
                for i, first in enumerate(firsts):
                    top = first * own
                    grd[top : top + own - 1, where] = source[8 * i : 8 * i + 8, where]
            return 0

        lax.fori_loop(0, own - 1, columns, 0)
        gone = [pltpu.make_async_copy(grd, grd_out, sems.at[0])]
        gone[0].start()
        g[...] = jnp.zeros_like(g)

        def grad_part(b, _):
            g[...] += jnp.dot(grd[:, at(b)], wt[b, :, 2 * hid :], preferred_element_type=F32)
            return 0

        lax.fori_loop(0, 4, grad_part, 0)
        for dz in range(N_Z):
            gate_pre, up_pre = pre[spot(dz), :, :hid], pre[spot(dz), :, hid:]
            rows = [slice((dy * N_Z + dz) * unit, (dy * N_Z + dz + 1) * unit) for dy in range(N_Y)]
            grad = jnp.concatenate([g[r, :] for r in rows], axis=0)
            sigma = jax.nn.sigmoid(gate_pre)
            swish = gate_pre * sigma
            hidden = (swish * up_pre).astype(BF)
            up_grad = (grad * swish).astype(BF)
            gate_grad = (grad * up_pre * sigma * (1.0 + gate_pre * (1.0 - sigma))).astype(BF)
            both = jnp.concatenate([gate_grad, up_grad], axis=1)
            first_ref[spot(dz)] = both
            by_z[dz * block : (dz + 1) * block, :] = both
            for dy in range(N_Y):
                hidden_ref[rows[dy], :] = hidden[dy * unit : (dy + 1) * unit]
        gone.append(pltpu.make_async_copy(first_ref, first_out, sems.at[1]))
        gone.append(pltpu.make_async_copy(hidden_ref, hidden_out, sems.at[2]))
        for copy in gone[1:]:
            copy.start()
        for copy in come_w:
            copy.wait()

        def send(b, dz):
            there = out.at[spot(dz), :, pl.ds(pl.multiple_of(b * cols, cols), cols)]
            return pltpu.make_async_copy(held.at[b, dz], there, out_sems.at[b, dz])

        def spread_part(b, _):
            part = jnp.dot(by_z[...], w[b], preferred_element_type=F32).astype(BF)
            for dz in range(N_Z):
                held[b, dz] = part[dz * block : (dz + 1) * block]
                send(b, dz).start()
            return 0

        lax.fori_loop(0, 4, spread_part, 0)

        def sent(i, _):
            send(i // N_Z, i % N_Z).wait()
            return 0

        lax.fori_loop(0, 4 * N_Z, sent, 0)
        for copy in gone:
            copy.wait()

    first, grd, hidden, sums = call(
        kernel,
        [
            jax.ShapeDtypeStruct((N_Z, block, 2 * hid), BF),
            jax.ShapeDtypeStruct((total, width), BF),
            jax.ShapeDtypeStruct((total, hid), BF),
            jax.ShapeDtypeStruct((N_Z, block, width), BF),
        ],
        [SCALARS] * 2 + [ANYWHERE] * (n + 13),
        8 * total * width + 12 * hid * width,
        flops=10 * total * hid * width,
        limit=BIG_LIMIT,
        out_specs=[ANYWHERE] * 4,
        scratch_shapes=[
            pltpu.VMEM((8 * len(firsts), width + tail), BF) for firsts, _ in pieces
        ]
        + [
            pltpu.VMEM((4, total, cols), BF),
            pltpu.VMEM((4, cols, 3 * hid), BF),
            pltpu.VMEM((4, 2 * hid, cols), BF),
            pltpu.VMEM((total, width), BF),
            pltpu.VMEM((total, hid), F32),
            pltpu.VMEM((total, 2 * hid), F32),
            pltpu.VMEM((N_Z, block, 2 * hid), F32),
            pltpu.VMEM((total, 2 * hid), BF),
            pltpu.VMEM((N_Z, block, 2 * hid), BF),
            pltpu.VMEM((total, hid), BF),
            pltpu.VMEM((4, N_Z, block, cols), BF),
            pltpu.SemaphoreType.DMA((n + 16,)),
            pltpu.SemaphoreType.DMA((4, N_Z)),
        ],
    )(z, place, tok, *flat, *turned, *[half for pair in blocks for half in pair])
    return first.reshape(total, 2 * hid), grd, hidden, sums.reshape(total, width)


def weight_grads(order, lefts, rights):
    hid, cols, n = lefts[0].shape[1], rights[0].shape[1] // 4, len(lefts)
    rows = lefts[0].shape[0]

    def kernel(order_ref, *refs):
        give_ref, keep_ref, held, left_ref, turned_ref, sems, left_sems = refs[2 * n :]
        come = [
            pltpu.make_async_copy(ref, left_ref.at[i], left_sems.at[i])
            for i, ref in enumerate(refs[:n])
        ]
        for copy in come:
            copy.start()
        for b in range(4):
            where = pl.ds(pl.multiple_of(order_ref[b] * cols, cols), cols)
            for i, right in enumerate(refs[n : 2 * n]):
                there = held.at[b, i * rows : (i + 1) * rows, :]
                pltpu.make_async_copy(right.at[:, where], there, sems.at[b, i]).start()
        for copy in come:
            copy.wait()
        turned_ref[...] = jnp.concatenate([left_ref[i] for i in range(n)], axis=0).T

        def column_part(b, _):
            for i, right in enumerate(refs[n : 2 * n]):
                there = held.at[b, i * rows : (i + 1) * rows, :]
                pltpu.make_async_copy(right.at[:, :cols], there, sems.at[b, i]).wait()
            part = jnp.dot(turned_ref[...], held[b], preferred_element_type=F32)

            @pl.when(b < 2)
            def _():
                give_ref[b] = part.astype(BF)

            @pl.when(b >= 2)
            def _():
                keep_ref[b - 2] = part

            return 0

        lax.fori_loop(0, 4, column_part, 0)

    return call(
        kernel,
        [jax.ShapeDtypeStruct((2, hid, cols), BF), jax.ShapeDtypeStruct((2, hid, cols), F32)],
        [SCALARS] + [ANYWHERE] * (2 * n),
        12 * hid * cols + 8 * n * rows * cols,
        flops=8 * n * rows * hid * cols,
        limit=BIG_LIMIT,
        scratch_shapes=[
            pltpu.VMEM((4, n * rows, cols), BF),
            pltpu.VMEM((n, rows, hid), BF),
            pltpu.VMEM((hid, n * rows), BF),
            pltpu.SemaphoreType.DMA((4, n)),
            pltpu.SemaphoreType.DMA((n,)),
        ],
    )(order, *lefts, *rights)


def per_device(tokens, out_grad, gate_weight, up_weight, down_weight, block_mask, assignment):
    own, width = tokens.shape
    hid, cols = gate_weight.shape
    panels, col_blocks = hid // BLK, cols // BLK
    unit = 2 * own
    x_hi, core, z = (lax.axis_index(a) for a in ("x_hi", "core", "z"))
    place = jnp.stack(
        [2 * x_hi + core, 2 * (1 - x_hi) + core, 2 * x_hi + 1 - core, 2 * (1 - x_hi) + 1 - core]
    )
    tie = lax.optimization_barrier

    panel_ids = lax.broadcasted_iota(jnp.int32, (panels, block_mask.shape[1]), 1)
    selector = (assignment[:, None] == panel_ids).astype(F32)
    slot_mask = jnp.einsum("sp,mpb->msb", selector, block_mask.astype(F32))
    slot_mask = lax.dynamic_slice_in_dim(slot_mask, place[0] * col_blocks, col_blocks, 2)
    keep = jnp.repeat(slot_mask, BLK, axis=2)

    mine = pack([tokens, out_grad])
    tok16, grd16 = by_array(mine, fetch(mine, "x_lo", 1))
    kept = mask_weights([gate_weight, up_weight, down_weight], keep.reshape(-1, cols))
    tok16, grd16, kept = tie((tok16, grd16, kept))

    t1, t3, t2 = fetch(tok16, "y", 1), fetch(tok16, "y", -1), fetch(tok16, "y", 2)
    z1, z7 = fetch(grd16, "z", 1), fetch(grd16, "z", -1)
    z1, z7, t1, t3, t2 = tie((z1, z7, t1, t3, t2))
    tok = unpack(
        [([2 * dy, 2 * dy + 1], [t]) for dy, t in enumerate((tok16, t1, t2, t3))], N_X * N_Y, own, width
    )
    tok = lax.all_gather(tok, "z", axis=0, tiled=True)
    away = [fetch(kept[0], "x_hi", 1)]
    beside_kept = [fetch(half, "core", 1) for half in kept]
    z2, z6, beside_kept = tie((fetch(z1, "z", 1), fetch(z7, "z", -1), beside_kept))
    near = stack([grd16, z1, z7, z2, z6])
    cut = near.shape[1] // 2
    n1, n3 = fetch(near, "y", 1), fetch(near, "y", -1)
    z3, z5 = tie((fetch(z2, "z", 1), fetch(z6, "z", -1)))
    z4 = [fetch(z3[:, :cut], "z", 1), fetch(z5[:, cut:], "z", -1)]
    z4, later = tie((z4, kept[1]))
    rest = join([[z3], [z5], z4])
    kept_turned = turn(kept)
    n1, n3, rest, kept_turned, away = tie((n1, n3, rest, kept_turned, away))
    n2 = [fetch(n1[:, :cut], "y", 1), fetch(n3[:, cut:], "y", -1)]
    r1, r3 = fetch(rest, "y", 1), fetch(rest, "y", -1)
    away = [away[0], fetch(later, "x_hi", 1)]
    n2, r1, r3, away, beside_turned = tie((n2, r1, r3, away, turn(beside_kept)))
    r2 = [fetch(r1[:, :cut], "y", 1), fetch(r3[:, cut:], "y", -1)]
    beside_away = [fetch(half, "core", 1) for half in away]
    blocks = [kept, away, beside_kept, beside_away]
    turned = [kept_turned, turn(away), beside_turned, turn(beside_away)]
    tok, r2, turned = tie((tok, r2, turned))
    pieces = []
    for dy, n, r in ((0, [near], [rest]), (1, [n1], [r1]), (2, n2, r2), (3, [n3], [r3])):
        for offsets, held in (((0, 1, 7, 2, 6), n), ((3, 5, 4), r)):
            pieces.append(([2 * (N_Z * dy + dz) + dx for dz in offsets for dx in range(N_X)], held))
    by_z, grd, hidden, total = middle(z[None], place, tok, pieces, turned, blocks, own)
    total = lax.psum_scatter(total, "z", scatter_dimension=0, tiled=True)

    order = place[::-1]
    give_a, keep_a = weight_grads(order, [by_z], [tok])
    give_a = fetch(give_a, "core", 1)
    give_b, keep_b = weight_grads(order, [hidden], [grd])
    give_a, give_b, keep_b = tie((give_a, give_b, keep_b))
    far_a = fetch((keep_a[0] + give_a[0].astype(F32)).astype(BF), "x_hi", 1)
    give_b = fetch(give_b, "core", 1)
    far_b = fetch((keep_b[0] + give_b[0].astype(F32)).astype(BF), "x_hi", 1)

    def finish(keep_sum, give, far, rows):
        total = keep_sum[1] + give[1].astype(F32) + far.astype(F32)
        total = total.reshape(-1, panels, BLK, cols) * rows[:, :, None, :]
        return total.astype(BF).reshape(-1, hid, cols)

    gate_up_grad = finish(keep_a, give_a, far_a, keep[:2])
    down_grad = finish(keep_b, give_b, far_b, keep[2:])

    parts = deal(total, own)
    parts = [parts[0]] + [fetch(parts[dy], "y", -dy) for dy in (1, 3, 2)]

    def last(*parts):
        both = sum(part.astype(F32) for part in parts)
        return both[: own - 1], both[own - 1 :]

    parts, gate_up_grad, down_grad = tie((parts, gate_up_grad, down_grad))
    mine, other = local(last, *parts)
    input_grad = place_rows(place, mine, fetch(other, "x_lo", 1))
    return (input_grad, gate_up_grad[0], gate_up_grad[1], down_grad[0])


def solution(mesh):
    fine = Mesh(mesh.devices.reshape(SIZES), AXES)
    rows = P(DP + MP, None)
    weights = P(MP, DP)
    return jax.shard_map(
        per_device,
        mesh=fine,
        in_specs=(rows, rows, weights, weights, weights, P(), P(MP)),
        out_specs=(rows, weights, weights, weights),
        check_vma=False,
    )
```

```python
import jax
import jax.numpy as jnp
from jax import lax
from jax.experimental import pallas as pl
from jax.experimental.pallas import tpu as pltpu
from jax.sharding import Mesh
from jax.sharding import PartitionSpec as P

BLK = 128
AXES = ("x_hi", "core", "x_lo", "y", "z")
SIZES = (2, 2, 2, 4, 8)
DP = ("x_hi", "core")
MP = ("x_lo", "y", "z")
N_X, N_Y, N_Z = 2, 4, 8
BF = jnp.bfloat16
F32 = jnp.float32
WHOLE = pl.BlockSpec(memory_space=pltpu.VMEM)
VMEM_LIMIT = 6 << 20
BIG_LIMIT = 52 << 20
ANYWHERE = pl.BlockSpec(memory_space=pl.ANY)
SCALARS = pl.BlockSpec(memory_space=pltpu.SMEM)


def call(kernel, out_shape, in_specs, bytes_accessed, flops=0, **more):
    return pl.pallas_call(
        kernel,
        out_shape=out_shape,
        in_specs=in_specs,
        out_specs=more.pop("out_specs", jax.tree.map(lambda _: WHOLE, out_shape)),
        compiler_params=pltpu.CompilerParams(vmem_limit_bytes=more.pop("limit", VMEM_LIMIT)),
        cost_estimate=pl.CostEstimate(
            flops=flops, bytes_accessed=bytes_accessed, transcendentals=0
        ),
        **more,
    )


def local(function, *arrays):
    out = jax.eval_shape(function, *arrays)

    def kernel(*refs):
        results = function(*(ref[...] for ref in refs[: len(arrays)]))
        for ref, value in zip(refs[len(arrays) :], results):
            ref[...] = value

    size = sum(a.size * a.dtype.itemsize for a in (*arrays, *out))
    return call(kernel, list(out), [WHOLE] * len(arrays), size)(*arrays)


def fetch(block, axis, offset):
    size = SIZES[AXES.index(axis)]
    return lax.ppermute(block, axis, [(i, (i - offset) % size) for i in range(size)])


def pack(arrays):
    own, width = arrays[0].shape
    tail, rows, n = width // (own - 1), own - 1, len(arrays)

    def kernel(*refs):
        out, held, sems = refs[n:]
        come = [pltpu.make_async_copy(refs[k], held.at[k], sems.at[k]) for k in range(n)]
        for copy in come:
            copy.start()
        for k in range(n):
            come[k].wait()
            out[k * rows : (k + 1) * rows, :width] = held[k, :rows, :]
            for i in range(rows):
                spot = k * rows + i
                part = held[k, rows : rows + 1, i * tail : (i + 1) * tail]
                out[spot : spot + 1, width:] = part

    return call(
        kernel,
        jax.ShapeDtypeStruct((rows * n, width + tail), BF),
        [ANYWHERE] * n,
        4 * own * width * n,
        limit=BIG_LIMIT,
        scratch_shapes=[pltpu.VMEM((n, own, width), BF), pltpu.SemaphoreType.DMA((n,))],
    )(*(pltpu.with_memory_space_constraint(a, pltpu.HBM) for a in arrays))


def by_array(mine, other):
    rows = mine.shape[0] // 2

    def kernel(mine_ref, other_ref, *out):
        for k in range(2):
            out[k][:rows, :] = mine_ref[k * rows : (k + 1) * rows, :]
            out[k][rows:, :] = other_ref[k * rows : (k + 1) * rows, :]

    out = [jax.ShapeDtypeStruct(mine.shape, BF)] * 2
    return call(kernel, out, [WHOLE] * 2, 4 * mine.shape[0] * mine.shape[1])(mine, other)


def stack(blocks):
    starts = [sum(b.shape[0] for b in blocks[:i]) for i in range(len(blocks) + 1)]

    def kernel(*refs):
        for ref, start in zip(refs[:-1], starts):
            refs[-1][start : start + ref.shape[0], :] = ref[...]

    whole = jax.ShapeDtypeStruct((starts[-1], blocks[0].shape[1]), blocks[0].dtype)
    size = 4 * starts[-1] * blocks[0].shape[1]
    return call(kernel, whole, [WHOLE] * len(blocks), size)(*blocks)


def join(lines):
    spots, flat, top = [], [], 0
    for line in lines:
        left = 0
        for block in line:
            spots.append((top, left))
            flat.append(block)
            left += block.shape[1]
        top += line[0].shape[0]

    def kernel(*refs):
        for ref, (row, col) in zip(refs[:-1], spots):
            refs[-1][row : row + ref.shape[0], col : col + ref.shape[1]] = ref[...]

    whole = jax.ShapeDtypeStruct((top, left), flat[0].dtype)
    return call(kernel, whole, [WHOLE] * len(flat), 4 * top * left)(*flat)


def unpack(pieces, units, own, width):
    tail = width // (own - 1)
    flat = [block for _, blocks in pieces for block in blocks]

    def kernel(*refs):
        out, at = refs[-1], 0
        for firsts, blocks in pieces:
            held = refs[at : at + len(blocks)]
            at += len(blocks)
            for i, unit in enumerate(firsts):
                rows = slice(8 * i, 8 * i + 8)
                top = unit * own
                value = jnp.concatenate([ref[rows, :] for ref in held], axis=1)
                out[top : top + own - 1, :] = value[:, :width]
                for j in range(own - 1):
                    part = value[j : j + 1, width:]
                    out[top + own - 1 : top + own, j * tail : (j + 1) * tail] = part

    whole = jax.ShapeDtypeStruct((units * own, width), BF)
    return call(kernel, whole, [WHOLE] * len(flat), 4 * units * own * width)(*flat)


def mask_weights(weights, keep_rows):
    rows, cols = weights[0].shape
    panels = rows // BLK

    def kernel(keep_ref, *refs):
        for m in range(len(weights)):
            for p in range(panels):
                row = m * panels + p
                keep = keep_ref[row : row + 1, :]
                kept = refs[m][p * BLK : (p + 1) * BLK, :].astype(F32) * keep
                half, row = divmod(row, len(weights) * panels // 2)
                refs[half - 2][row * BLK : (row + 1) * BLK, :] = kept.astype(BF)

    out = [jax.ShapeDtypeStruct((rows * len(weights) // 2, cols), BF)] * 2
    return call(kernel, out, [WHOLE] * 4, 12 * rows * cols)(keep_rows, *weights)


def turn(halves):
    rows, cols = halves[0].shape

    def kernel(top, bottom, out, held, turned, sems):
        come = [
            pltpu.make_async_copy(half, held.at[i], sems.at[i])
            for i, half in enumerate((top, bottom))
        ]
        for copy in come:
            copy.start()
        for i in range(2):
            come[i].wait()
            turned[:, i * rows : (i + 1) * rows] = held[i].T
        gone = pltpu.make_async_copy(turned, out, sems.at[2])
        gone.start()
        gone.wait()

    return call(
        kernel,
        jax.ShapeDtypeStruct((cols, 2 * rows), BF),
        [ANYWHERE] * 2,
        8 * rows * cols,
        limit=BIG_LIMIT,
        out_specs=ANYWHERE,
        scratch_shapes=[
            pltpu.VMEM((2, rows, cols), BF),
            pltpu.VMEM((cols, 2 * rows), BF),
            pltpu.SemaphoreType.DMA((3,)),
        ],
    )(*halves)


def deal(total, own):
    width = total.shape[1]
    unit, rows, tail = N_X * own, own - 1, width // (own - 1)
    count = total.shape[0] // unit

    def kernel(ref, *refs):
        out, held, sem = refs[:count], refs[count], refs[count + 1]
        come = pltpu.make_async_copy(ref, held, sem)
        come.start()
        come.wait()
        for u in range(count):
            for k in range(N_X):
                top = u * unit + k * own
                out[u][k * rows : (k + 1) * rows, :width] = held[top : top + rows, :]
                for i in range(rows):
                    part = held[top + rows : top + own, i * tail : (i + 1) * tail]
                    out[u][k * rows + i : k * rows + i + 1, width:] = part

    spec = [jax.ShapeDtypeStruct((N_X * rows, width + tail), BF)] * count
    return call(
        kernel,
        spec,
        [ANYWHERE],
        6 * total.shape[0] * width,
        scratch_shapes=[pltpu.VMEM(total.shape, BF), pltpu.SemaphoreType.DMA],
    )(pltpu.with_memory_space_constraint(total, pltpu.HBM))


def place_rows(place, mine, other):
    rows, packed = mine.shape
    width = packed * rows // (rows + 1)
    cols, tail = width // 4, width // rows

    def kernel(place_ref, mine_ref, other_ref, out):
        total = (mine_ref[...] + other_ref[...]).astype(BF)
        for b in range(4):
            start = place_ref[b] * cols
            where = pl.ds(pl.multiple_of(start, tail), cols)
            out[:rows, where] = total[:, b * cols : (b + 1) * cols]
            for j in range(cols // tail):
                i = b * (cols // tail) + j
                where = pl.ds(pl.multiple_of(start + j * tail, tail), tail)
                out[rows : rows + 1, where] = total[i : i + 1, width:]

    out = jax.ShapeDtypeStruct((rows + 1, width), BF)
    return call(kernel, out, [SCALARS, WHOLE, WHOLE], 10 * rows * packed)(place, mine, other)


def middle(z, place, tok, pieces, turned, blocks, own):
    total, width = tok.shape
    cut, cols = blocks[0][0].shape
    hid = 2 * cut // 3
    unit, tail = N_X * own, width // (own - 1)
    block = N_Y * unit
    flat = [part for _, held in pieces for part in held]
    n, m = len(flat), len(pieces)

    def kernel(z_ref, place_ref, tok_ref, *refs):
        piece_refs, turned_refs, block_refs = refs[:n], refs[n : n + 4], refs[n + 4 : n + 12]
        first_out, grd_out, hidden_out, out = refs[n + 12 : n + 16]
        packed = refs[n + 16 : n + 16 + m]
        x, wt, w, grd, g, total_ref, pre, by_z, first_ref, hidden_ref, held, sems, out_sems = refs[n + 16 + m :]

        def bring(source, target, i):
            copy = pltpu.make_async_copy(source, target, sems.at[i])
            copy.start()
            return copy

        def spot(dz):
            return lax.rem(z_ref[0] + dz, N_Z)

        def at(b):
            return pl.ds(pl.multiple_of(place_ref[b] * cols, cols), cols)

        for b in range(4):
            bring(turned_refs[b], wt.at[b], n + b)
            bring(tok_ref.at[:, at(b)], x.at[b], n + 4 + b)
        come, i = [], 0
        for target, (_, parts) in zip(packed, pieces):
            size = target.shape[1] // len(parts)
            for j in range(len(parts)):
                come.append(bring(piece_refs[i], target.at[:, j * size : (j + 1) * size], i))
                i += 1
        come_w = []
        for b in range(4):
            top, bottom = block_refs[2 * b], block_refs[2 * b + 1].at[: 2 * hid - cut, :]
            come_w.append(bring(top, w.at[b, :cut, :], n + 8 + b))
            come_w.append(bring(bottom, w.at[b, cut:, :], n + 12 + b))
        def pre_part(b, _):
            pltpu.make_async_copy(turned_refs[0], wt.at[b], sems.at[n + b]).wait()
            pltpu.make_async_copy(tok_ref.at[:, :cols], x.at[b], sems.at[n + 4 + b]).wait()
            part = jnp.dot(x[b], wt[b, :, : 2 * hid], preferred_element_type=F32)

            @pl.when(b == 0)
            def _():
                total_ref[...] = part

            @pl.when(b > 0)
            def _():
                total_ref[...] += part

            return 0

        lax.fori_loop(0, 4, pre_part, 0)
        for i in range(N_Z):
            pre[i] = total_ref[i * block : (i + 1) * block, :]
        for copy in come:
            copy.wait()
        for source, (firsts, _) in zip(packed, pieces):
            for i, first in enumerate(firsts):
                value = source[8 * i : 8 * i + 8, width:]
                top = first * own
                for j in range(own - 1):
                    spot_j = slice(j * tail, (j + 1) * tail)
                    grd[top + own - 1 : top + own, spot_j] = value[j : j + 1]

        def columns(c, _):
            where = pl.ds(pl.multiple_of(c * tail, tail), tail)
            for source, (firsts, _) in zip(packed, pieces):
                for i, first in enumerate(firsts):
                    top = first * own
                    grd[top : top + own - 1, where] = source[8 * i : 8 * i + 8, where]
            return 0

        lax.fori_loop(0, own - 1, columns, 0)
        gone = [pltpu.make_async_copy(grd, grd_out, sems.at[0])]
        gone[0].start()
        g[...] = jnp.zeros_like(g)

        def grad_part(b, _):
            g[...] += jnp.dot(grd[:, at(b)], wt[b, :, 2 * hid :], preferred_element_type=F32)
            return 0

        lax.fori_loop(0, 4, grad_part, 0)
        for dz in range(N_Z):
            gate_pre, up_pre = pre[spot(dz), :, :hid], pre[spot(dz), :, hid:]
            rows = [slice((dy * N_Z + dz) * unit, (dy * N_Z + dz + 1) * unit) for dy in range(N_Y)]
            grad = jnp.concatenate([g[r, :] for r in rows], axis=0)
            sigma = jax.nn.sigmoid(gate_pre)
            swish = gate_pre * sigma
            hidden = (swish * up_pre).astype(BF)
            up_grad = (grad * swish).astype(BF)
            gate_grad = (grad * up_pre * sigma * (1.0 + gate_pre * (1.0 - sigma))).astype(BF)
            both = jnp.concatenate([gate_grad, up_grad], axis=1)
            first_ref[spot(dz)] = both
            by_z[dz * block : (dz + 1) * block, :] = both
            for dy in range(N_Y):
                hidden_ref[rows[dy], :] = hidden[dy * unit : (dy + 1) * unit]
        gone.append(pltpu.make_async_copy(first_ref, first_out, sems.at[1]))
        gone.append(pltpu.make_async_copy(hidden_ref, hidden_out, sems.at[2]))
        for copy in gone[1:]:
            copy.start()
        for copy in come_w:
            copy.wait()

        def send(b, dz):
            there = out.at[spot(dz), :, pl.ds(pl.multiple_of(b * cols, cols), cols)]
            return pltpu.make_async_copy(held.at[b, dz], there, out_sems.at[b, dz])

        def spread_part(b, _):
            part = jnp.dot(by_z[...], w[b], preferred_element_type=F32).astype(BF)
            for dz in range(N_Z):
                held[b, dz] = part[dz * block : (dz + 1) * block]
                send(b, dz).start()
            return 0

        lax.fori_loop(0, 4, spread_part, 0)

        def sent(i, _):
            send(i // N_Z, i % N_Z).wait()
            return 0

        lax.fori_loop(0, 4 * N_Z, sent, 0)
        for copy in gone:
            copy.wait()

    first, grd, hidden, sums = call(
        kernel,
        [
            jax.ShapeDtypeStruct((N_Z, block, 2 * hid), BF),
            jax.ShapeDtypeStruct((total, width), BF),
            jax.ShapeDtypeStruct((total, hid), BF),
            jax.ShapeDtypeStruct((N_Z, block, width), BF),
        ],
        [SCALARS] * 2 + [ANYWHERE] * (n + 13),
        8 * total * width + 12 * hid * width,
        flops=10 * total * hid * width,
        limit=BIG_LIMIT,
        out_specs=[ANYWHERE] * 4,
        scratch_shapes=[
            pltpu.VMEM((8 * len(firsts), width + tail), BF) for firsts, _ in pieces
        ]
        + [
            pltpu.VMEM((4, total, cols), BF),
            pltpu.VMEM((4, cols, 3 * hid), BF),
            pltpu.VMEM((4, 2 * hid, cols), BF),
            pltpu.VMEM((total, width), BF),
            pltpu.VMEM((total, hid), F32),
            pltpu.VMEM((total, 2 * hid), F32),
            pltpu.VMEM((N_Z, block, 2 * hid), F32),
            pltpu.VMEM((total, 2 * hid), BF),
            pltpu.VMEM((N_Z, block, 2 * hid), BF),
            pltpu.VMEM((total, hid), BF),
            pltpu.VMEM((4, N_Z, block, cols), BF),
            pltpu.SemaphoreType.DMA((n + 16,)),
            pltpu.SemaphoreType.DMA((4, N_Z)),
        ],
    )(z, place, tok, *flat, *turned, *[half for pair in blocks for half in pair])
    return first.reshape(total, 2 * hid), grd, hidden, sums.reshape(total, width)


def weight_grads(order, lefts, rights):
    hid, cols, n = lefts[0].shape[1], rights[0].shape[1] // 4, len(lefts)
    rows = lefts[0].shape[0]

    def kernel(order_ref, *refs):
        give_ref, keep_ref, held, left_ref, turned_ref, sems, left_sems = refs[2 * n :]
        come = [
            pltpu.make_async_copy(ref, left_ref.at[i], left_sems.at[i])
            for i, ref in enumerate(refs[:n])
        ]
        for copy in come:
            copy.start()
        for b in range(4):
            where = pl.ds(pl.multiple_of(order_ref[b] * cols, cols), cols)
            for i, right in enumerate(refs[n : 2 * n]):
                there = held.at[b, i * rows : (i + 1) * rows, :]
                pltpu.make_async_copy(right.at[:, where], there, sems.at[b, i]).start()
        for copy in come:
            copy.wait()
        turned_ref[...] = jnp.concatenate([left_ref[i] for i in range(n)], axis=0).T

        def column_part(b, _):
            for i, right in enumerate(refs[n : 2 * n]):
                there = held.at[b, i * rows : (i + 1) * rows, :]
                pltpu.make_async_copy(right.at[:, :cols], there, sems.at[b, i]).wait()
            part = jnp.dot(turned_ref[...], held[b], preferred_element_type=F32)

            @pl.when(b < 2)
            def _():
                give_ref[b] = part.astype(BF)

            @pl.when(b >= 2)
            def _():
                keep_ref[b - 2] = part

            return 0

        lax.fori_loop(0, 4, column_part, 0)

    return call(
        kernel,
        [jax.ShapeDtypeStruct((2, hid, cols), BF), jax.ShapeDtypeStruct((2, hid, cols), F32)],
        [SCALARS] + [ANYWHERE] * (2 * n),
        12 * hid * cols + 8 * n * rows * cols,
        flops=8 * n * rows * hid * cols,
        limit=BIG_LIMIT,
        scratch_shapes=[
            pltpu.VMEM((4, n * rows, cols), BF),
            pltpu.VMEM((n, rows, hid), BF),
            pltpu.VMEM((hid, n * rows), BF),
            pltpu.SemaphoreType.DMA((4, n)),
            pltpu.SemaphoreType.DMA((n,)),
        ],
    )(order, *lefts, *rights)


def per_device(tokens, out_grad, gate_weight, up_weight, down_weight, block_mask, assignment):
    own, width = tokens.shape
    hid, cols = gate_weight.shape
    panels, col_blocks = hid // BLK, cols // BLK
    unit = 2 * own
    x_hi, core, z = (lax.axis_index(a) for a in ("x_hi", "core", "z"))
    place = jnp.stack(
        [2 * x_hi + core, 2 * (1 - x_hi) + core, 2 * x_hi + 1 - core, 2 * (1 - x_hi) + 1 - core]
    )
    tie = lax.optimization_barrier

    panel_ids = lax.broadcasted_iota(jnp.int32, (panels, block_mask.shape[1]), 1)
    selector = (assignment[:, None] == panel_ids).astype(F32)
    slot_mask = jnp.einsum("sp,mpb->msb", selector, block_mask.astype(F32))
    slot_mask = lax.dynamic_slice_in_dim(slot_mask, place[0] * col_blocks, col_blocks, 2)
    keep = jnp.repeat(slot_mask, BLK, axis=2)

    mine = pack([tokens, out_grad])
    tok16, grd16 = by_array(mine, fetch(mine, "x_lo", 1))
    kept = mask_weights([gate_weight, up_weight, down_weight], keep.reshape(-1, cols))
    tok16, grd16, kept = tie((tok16, grd16, kept))

    t1, t3, t2 = fetch(tok16, "y", 1), fetch(tok16, "y", -1), fetch(tok16, "y", 2)
    z1, z7 = fetch(grd16, "z", 1), fetch(grd16, "z", -1)
    z1, z7, t1, t3, t2 = tie((z1, z7, t1, t3, t2))
    tok = unpack(
        [([2 * dy, 2 * dy + 1], [t]) for dy, t in enumerate((tok16, t1, t2, t3))], N_X * N_Y, own, width
    )
    tok = lax.all_gather(tok, "z", axis=0, tiled=True)
    away = [fetch(kept[0], "x_hi", 1)]
    beside_kept = [fetch(half, "core", 1) for half in kept]
    z2, z6, beside_kept = tie((fetch(z1, "z", 1), fetch(z7, "z", -1), beside_kept))
    near = stack([grd16, z1, z7, z2, z6])
    cut = near.shape[1] // 2
    n1, n3 = fetch(near, "y", 1), fetch(near, "y", -1)
    z3, z5 = tie((fetch(z2, "z", 1), fetch(z6, "z", -1)))
    z4 = [fetch(z3[:, :cut], "z", 1), fetch(z5[:, cut:], "z", -1)]
    z4, later = tie((z4, kept[1]))
    rest = join([[z3], [z5], z4])
    n1, n3, rest, away = tie((n1, n3, rest, away))
    n2 = [fetch(n1[:, :cut], "y", 1), fetch(n3[:, cut:], "y", -1)]
    r1, r3 = fetch(rest, "y", 1), fetch(rest, "y", -1)
    away = [away[0], fetch(later, "x_hi", 1)]
    kept_turned, beside_turned = turn(kept), turn(beside_kept)
    n2, r1, r3, away, kept_turned, beside_turned = tie(
        (n2, r1, r3, away, kept_turned, beside_turned)
    )
    r2 = [fetch(r1[:, :cut], "y", 1), fetch(r3[:, cut:], "y", -1)]
    beside_away = [fetch(half, "core", 1) for half in away]
    blocks = [kept, away, beside_kept, beside_away]
    turned = [kept_turned, turn(away), beside_turned, turn(beside_away)]
    tok, r2, turned = tie((tok, r2, turned))
    pieces = []
    for dy, n, r in ((0, [near], [rest]), (1, [n1], [r1]), (2, n2, r2), (3, [n3], [r3])):
        for offsets, held in (((0, 1, 7, 2, 6), n), ((3, 5, 4), r)):
            pieces.append(([2 * (N_Z * dy + dz) + dx for dz in offsets for dx in range(N_X)], held))
    by_z, grd, hidden, total = middle(z[None], place, tok, pieces, turned, blocks, own)
    total = lax.psum_scatter(total, "z", scatter_dimension=0, tiled=True)

    order = place[::-1]
    give_a, keep_a = weight_grads(order, [by_z], [tok])
    give_a = fetch(give_a, "core", 1)
    give_b, keep_b = weight_grads(order, [hidden], [grd])
    give_a, give_b, keep_b = tie((give_a, give_b, keep_b))
    far_a = fetch((keep_a[0] + give_a[0].astype(F32)).astype(BF), "x_hi", 1)
    give_b = fetch(give_b, "core", 1)
    far_b = fetch((keep_b[0] + give_b[0].astype(F32)).astype(BF), "x_hi", 1)

    def finish(keep_sum, give, far, rows):
        total = keep_sum[1] + give[1].astype(F32) + far.astype(F32)
        total = total.reshape(-1, panels, BLK, cols) * rows[:, :, None, :]
        return total.astype(BF).reshape(-1, hid, cols)

    gate_up_grad = finish(keep_a, give_a, far_a, keep[:2])
    down_grad = finish(keep_b, give_b, far_b, keep[2:])

    parts = deal(total, own)
    parts = [parts[0]] + [fetch(parts[dy], "y", -dy) for dy in (1, 3, 2)]

    def last(*parts):
        both = sum(part.astype(F32) for part in parts)
        return both[: own - 1], both[own - 1 :]

    parts, gate_up_grad, down_grad = tie((parts, gate_up_grad, down_grad))
    mine, other = local(last, *parts)
    input_grad = place_rows(place, mine, fetch(other, "x_lo", 1))
    return (input_grad, gate_up_grad[0], gate_up_grad[1], down_grad[0])


def solution(mesh):
    fine = Mesh(mesh.devices.reshape(SIZES), AXES)
    rows = P(DP + MP, None)
    weights = P(MP, DP)
    return jax.shard_map(
        per_device,
        mesh=fine,
        in_specs=(rows, rows, weights, weights, weights, P(), P(MP)),
        out_specs=(rows, weights, weights, weights),
        check_vma=False,
    )
```

```python
import jax
import jax.numpy as jnp
from jax import lax
from jax.experimental import pallas as pl
from jax.experimental.pallas import tpu as pltpu
from jax.sharding import Mesh
from jax.sharding import PartitionSpec as P

BLK = 128
AXES = ("x_hi", "core", "x_lo", "y", "z")
SIZES = (2, 2, 2, 4, 8)
DP = ("x_hi", "core")
MP = ("x_lo", "y", "z")
N_X, N_Y, N_Z = 2, 4, 8
BF = jnp.bfloat16
F32 = jnp.float32
WHOLE = pl.BlockSpec(memory_space=pltpu.VMEM)
VMEM_LIMIT = 6 << 20
BIG_LIMIT = 52 << 20
ANYWHERE = pl.BlockSpec(memory_space=pl.ANY)
SCALARS = pl.BlockSpec(memory_space=pltpu.SMEM)


def call(kernel, out_shape, in_specs, bytes_accessed, flops=0, **more):
    return pl.pallas_call(
        kernel,
        out_shape=out_shape,
        in_specs=in_specs,
        out_specs=more.pop("out_specs", jax.tree.map(lambda _: WHOLE, out_shape)),
        compiler_params=pltpu.CompilerParams(vmem_limit_bytes=more.pop("limit", VMEM_LIMIT)),
        cost_estimate=pl.CostEstimate(
            flops=flops, bytes_accessed=bytes_accessed, transcendentals=0
        ),
        **more,
    )


def local(function, *arrays):
    out = jax.eval_shape(function, *arrays)

    def kernel(*refs):
        results = function(*(ref[...] for ref in refs[: len(arrays)]))
        for ref, value in zip(refs[len(arrays) :], results):
            ref[...] = value

    size = sum(a.size * a.dtype.itemsize for a in (*arrays, *out))
    return call(kernel, list(out), [WHOLE] * len(arrays), size)(*arrays)


def fetch(block, axis, offset):
    size = SIZES[AXES.index(axis)]
    return lax.ppermute(block, axis, [(i, (i - offset) % size) for i in range(size)])


def pack(arrays):
    own, width = arrays[0].shape
    tail, rows, n = width // (own - 1), own - 1, len(arrays)

    def kernel(*refs):
        out, held, sems = refs[n:]
        come = [pltpu.make_async_copy(refs[k], held.at[k], sems.at[k]) for k in range(n)]
        for copy in come:
            copy.start()
        for k in range(n):
            come[k].wait()
            out[k * rows : (k + 1) * rows, :width] = held[k, :rows, :]
            for i in range(rows):
                spot = k * rows + i
                part = held[k, rows : rows + 1, i * tail : (i + 1) * tail]
                out[spot : spot + 1, width:] = part

    return call(
        kernel,
        jax.ShapeDtypeStruct((rows * n, width + tail), BF),
        [ANYWHERE] * n,
        4 * own * width * n,
        limit=BIG_LIMIT,
        scratch_shapes=[pltpu.VMEM((n, own, width), BF), pltpu.SemaphoreType.DMA((n,))],
    )(*(pltpu.with_memory_space_constraint(a, pltpu.HBM) for a in arrays))


def by_array(mine, other):
    rows = mine.shape[0] // 2

    def kernel(mine_ref, other_ref, *out):
        for k in range(2):
            out[k][:rows, :] = mine_ref[k * rows : (k + 1) * rows, :]
            out[k][rows:, :] = other_ref[k * rows : (k + 1) * rows, :]

    out = [jax.ShapeDtypeStruct(mine.shape, BF)] * 2
    return call(kernel, out, [WHOLE] * 2, 4 * mine.shape[0] * mine.shape[1])(mine, other)


def stack(blocks):
    starts = [sum(b.shape[0] for b in blocks[:i]) for i in range(len(blocks) + 1)]

    def kernel(*refs):
        for ref, start in zip(refs[:-1], starts):
            refs[-1][start : start + ref.shape[0], :] = ref[...]

    whole = jax.ShapeDtypeStruct((starts[-1], blocks[0].shape[1]), blocks[0].dtype)
    size = 4 * starts[-1] * blocks[0].shape[1]
    return call(kernel, whole, [WHOLE] * len(blocks), size)(*blocks)


def join(lines):
    spots, flat, top = [], [], 0
    for line in lines:
        left = 0
        for block in line:
            spots.append((top, left))
            flat.append(block)
            left += block.shape[1]
        top += line[0].shape[0]

    def kernel(*refs):
        for ref, (row, col) in zip(refs[:-1], spots):
            refs[-1][row : row + ref.shape[0], col : col + ref.shape[1]] = ref[...]

    whole = jax.ShapeDtypeStruct((top, left), flat[0].dtype)
    return call(kernel, whole, [WHOLE] * len(flat), 4 * top * left)(*flat)


def unpack(pieces, units, own, width):
    tail = width // (own - 1)
    flat = [block for _, blocks in pieces for block in blocks]

    def kernel(*refs):
        out, at = refs[-1], 0
        for firsts, blocks in pieces:
            held = refs[at : at + len(blocks)]
            at += len(blocks)
            for i, unit in enumerate(firsts):
                rows = slice(8 * i, 8 * i + 8)
                top = unit * own
                value = jnp.concatenate([ref[rows, :] for ref in held], axis=1)
                out[top : top + own - 1, :] = value[:, :width]
                for j in range(own - 1):
                    part = value[j : j + 1, width:]
                    out[top + own - 1 : top + own, j * tail : (j + 1) * tail] = part

    whole = jax.ShapeDtypeStruct((units * own, width), BF)
    return call(kernel, whole, [WHOLE] * len(flat), 4 * units * own * width)(*flat)


def mask_weights(weights, keep_rows):
    rows, cols = weights[0].shape
    panels = rows // BLK

    def kernel(keep_ref, *refs):
        for m in range(len(weights)):
            for p in range(panels):
                row = m * panels + p
                keep = keep_ref[row : row + 1, :]
                kept = refs[m][p * BLK : (p + 1) * BLK, :].astype(F32) * keep
                half, row = divmod(row, len(weights) * panels // 2)
                refs[half - 2][row * BLK : (row + 1) * BLK, :] = kept.astype(BF)

    out = [jax.ShapeDtypeStruct((rows * len(weights) // 2, cols), BF)] * 2
    return call(kernel, out, [WHOLE] * 4, 12 * rows * cols)(keep_rows, *weights)


def turn(halves):
    rows, cols = halves[0].shape

    def kernel(top, bottom, out, held, turned, sems):
        come = [
            pltpu.make_async_copy(half, held.at[i], sems.at[i])
            for i, half in enumerate((top, bottom))
        ]
        for copy in come:
            copy.start()
        for i in range(2):
            come[i].wait()
            turned[:, i * rows : (i + 1) * rows] = held[i].T
        gone = pltpu.make_async_copy(turned, out, sems.at[2])
        gone.start()
        gone.wait()

    return call(
        kernel,
        jax.ShapeDtypeStruct((cols, 2 * rows), BF),
        [ANYWHERE] * 2,
        8 * rows * cols,
        limit=BIG_LIMIT,
        out_specs=ANYWHERE,
        scratch_shapes=[
            pltpu.VMEM((2, rows, cols), BF),
            pltpu.VMEM((cols, 2 * rows), BF),
            pltpu.SemaphoreType.DMA((3,)),
        ],
    )(*halves)


def deal(total, own):
    width = total.shape[1]
    unit, rows, tail = N_X * own, own - 1, width // (own - 1)
    count = total.shape[0] // unit

    def kernel(ref, *refs):
        out, held, sem = refs[:count], refs[count], refs[count + 1]
        come = pltpu.make_async_copy(ref, held, sem)
        come.start()
        come.wait()
        for u in range(count):
            for k in range(N_X):
                top = u * unit + k * own
                out[u][k * rows : (k + 1) * rows, :width] = held[top : top + rows, :]
                for i in range(rows):
                    part = held[top + rows : top + own, i * tail : (i + 1) * tail]
                    out[u][k * rows + i : k * rows + i + 1, width:] = part

    spec = [jax.ShapeDtypeStruct((N_X * rows, width + tail), BF)] * count
    return call(
        kernel,
        spec,
        [ANYWHERE],
        6 * total.shape[0] * width,
        scratch_shapes=[pltpu.VMEM(total.shape, BF), pltpu.SemaphoreType.DMA],
    )(pltpu.with_memory_space_constraint(total, pltpu.HBM))


def place_rows(place, mine, other):
    rows, packed = mine.shape
    width = packed * rows // (rows + 1)
    cols, tail = width // 4, width // rows

    def kernel(place_ref, mine_ref, other_ref, out):
        total = (mine_ref[...] + other_ref[...]).astype(BF)
        for b in range(4):
            start = place_ref[b] * cols
            where = pl.ds(pl.multiple_of(start, tail), cols)
            out[:rows, where] = total[:, b * cols : (b + 1) * cols]
            for j in range(cols // tail):
                i = b * (cols // tail) + j
                where = pl.ds(pl.multiple_of(start + j * tail, tail), tail)
                out[rows : rows + 1, where] = total[i : i + 1, width:]

    out = jax.ShapeDtypeStruct((rows + 1, width), BF)
    return call(kernel, out, [SCALARS, WHOLE, WHOLE], 10 * rows * packed)(place, mine, other)


def middle(z, place, tok, pieces, turned, blocks, own):
    total, width = tok.shape
    cut, cols = blocks[0][0].shape
    hid = 2 * cut // 3
    unit, tail = N_X * own, width // (own - 1)
    block = N_Y * unit
    flat = [part for _, held in pieces for part in held]
    n, m = len(flat), len(pieces)

    def kernel(z_ref, place_ref, tok_ref, *refs):
        piece_refs, turned_refs, block_refs = refs[:n], refs[n : n + 4], refs[n + 4 : n + 12]
        first_out, grd_out, hidden_out, out = refs[n + 12 : n + 16]
        packed = refs[n + 16 : n + 16 + m]
        x, wt, w, grd, g, total_ref, by_z, first_ref, hidden_ref, held, sems, out_sems = refs[n + 16 + m :]

        def bring(source, target, i):
            copy = pltpu.make_async_copy(source, target, sems.at[i])
            copy.start()
            return copy

        def spot(dz):
            return lax.rem(z_ref[0] + dz, N_Z)

        def at(b):
            return pl.ds(pl.multiple_of(place_ref[b] * cols, cols), cols)

        for b in range(4):
            bring(turned_refs[b], wt.at[b], n + b)
            bring(tok_ref.at[:, at(b)], x.at[b], n + 4 + b)
        come, i = [], 0
        for target, (_, parts) in zip(packed, pieces):
            size = target.shape[1] // len(parts)
            for j in range(len(parts)):
                come.append(bring(piece_refs[i], target.at[:, j * size : (j + 1) * size], i))
                i += 1
        come_w = []
        for b in range(4):
            top, bottom = block_refs[2 * b], block_refs[2 * b + 1].at[: 2 * hid - cut, :]
            come_w.append(bring(top, w.at[b, :cut, :], n + 8 + b))
            come_w.append(bring(bottom, w.at[b, cut:, :], n + 12 + b))
        def pre_part(b, _):
            pltpu.make_async_copy(turned_refs[0], wt.at[b], sems.at[n + b]).wait()
            pltpu.make_async_copy(tok_ref.at[:, :cols], x.at[b], sems.at[n + 4 + b]).wait()
            part = jnp.dot(x[b], wt[b, :, : 2 * hid], preferred_element_type=F32)

            @pl.when(b == 0)
            def _():
                total_ref[...] = part

            @pl.when(b > 0)
            def _():
                total_ref[...] += part

            return 0

        lax.fori_loop(0, 4, pre_part, 0)
        for copy in come:
            copy.wait()
        for source, (firsts, _) in zip(packed, pieces):
            for i, first in enumerate(firsts):
                value = source[8 * i : 8 * i + 8, width:]
                top = first * own
                for j in range(own - 1):
                    spot_j = slice(j * tail, (j + 1) * tail)
                    grd[top + own - 1 : top + own, spot_j] = value[j : j + 1]

        def columns(c, _):
            where = pl.ds(pl.multiple_of(c * tail, tail), tail)
            for source, (firsts, _) in zip(packed, pieces):
                for i, first in enumerate(firsts):
                    top = first * own
                    grd[top : top + own - 1, where] = source[8 * i : 8 * i + 8, where]
            return 0

        lax.fori_loop(0, own - 1, columns, 0)
        gone = [pltpu.make_async_copy(grd, grd_out, sems.at[0])]
        gone[0].start()
        g[...] = jnp.zeros_like(g)

        def grad_part(b, _):
            g[...] += jnp.dot(grd[:, at(b)], wt[b, :, 2 * hid :], preferred_element_type=F32)
            return 0

        lax.fori_loop(0, 4, grad_part, 0)
        for dz in range(N_Z):
            held_rows = pl.ds(pl.multiple_of(spot(dz) * block, block), block)
            gate_pre, up_pre = total_ref[held_rows, :hid], total_ref[held_rows, hid:]
            rows = [slice((dy * N_Z + dz) * unit, (dy * N_Z + dz + 1) * unit) for dy in range(N_Y)]
            grad = jnp.concatenate([g[r, :] for r in rows], axis=0)
            sigma = jax.nn.sigmoid(gate_pre)
            swish = gate_pre * sigma
            hidden = (swish * up_pre).astype(BF)
            up_grad = (grad * swish).astype(BF)
            gate_grad = (grad * up_pre * sigma * (1.0 + gate_pre * (1.0 - sigma))).astype(BF)
            both = jnp.concatenate([gate_grad, up_grad], axis=1)
            first_ref[spot(dz)] = both
            by_z[dz * block : (dz + 1) * block, :] = both
            for dy in range(N_Y):
                hidden_ref[rows[dy], :] = hidden[dy * unit : (dy + 1) * unit]
        gone.append(pltpu.make_async_copy(first_ref, first_out, sems.at[1]))
        gone.append(pltpu.make_async_copy(hidden_ref, hidden_out, sems.at[2]))
        for copy in gone[1:]:
            copy.start()
        for copy in come_w:
            copy.wait()

        def send(b, dz):
            there = out.at[spot(dz), :, pl.ds(pl.multiple_of(b * cols, cols), cols)]
            return pltpu.make_async_copy(held.at[b, dz], there, out_sems.at[b, dz])

        def spread_part(b, _):
            part = jnp.dot(by_z[...], w[b], preferred_element_type=F32).astype(BF)
            for dz in range(N_Z):
                held[b, dz] = part[dz * block : (dz + 1) * block]
                send(b, dz).start()
            return 0

        lax.fori_loop(0, 4, spread_part, 0)

        def sent(i, _):
            send(i // N_Z, i % N_Z).wait()
            return 0

        lax.fori_loop(0, 4 * N_Z, sent, 0)
        for copy in gone:
            copy.wait()

    first, grd, hidden, sums = call(
        kernel,
        [
            jax.ShapeDtypeStruct((N_Z, block, 2 * hid), BF),
            jax.ShapeDtypeStruct((total, width), BF),
            jax.ShapeDtypeStruct((total, hid), BF),
            jax.ShapeDtypeStruct((N_Z, block, width), BF),
        ],
        [SCALARS] * 2 + [ANYWHERE] * (n + 13),
        8 * total * width + 12 * hid * width,
        flops=10 * total * hid * width,
        limit=BIG_LIMIT,
        out_specs=[ANYWHERE] * 4,
        scratch_shapes=[
            pltpu.VMEM((8 * len(firsts), width + tail), BF) for firsts, _ in pieces
        ]
        + [
            pltpu.VMEM((4, total, cols), BF),
            pltpu.VMEM((4, cols, 3 * hid), BF),
            pltpu.VMEM((4, 2 * hid, cols), BF),
            pltpu.VMEM((total, width), BF),
            pltpu.VMEM((total, hid), F32),
            pltpu.VMEM((total, 2 * hid), F32),
            pltpu.VMEM((total, 2 * hid), BF),
            pltpu.VMEM((N_Z, block, 2 * hid), BF),
            pltpu.VMEM((total, hid), BF),
            pltpu.VMEM((4, N_Z, block, cols), BF),
            pltpu.SemaphoreType.DMA((n + 16,)),
            pltpu.SemaphoreType.DMA((4, N_Z)),
        ],
    )(z, place, tok, *flat, *turned, *[half for pair in blocks for half in pair])
    return first.reshape(total, 2 * hid), grd, hidden, sums.reshape(total, width)


def weight_grads(order, lefts, rights):
    hid, cols, n = lefts[0].shape[1], rights[0].shape[1] // 4, len(lefts)
    rows = lefts[0].shape[0]

    def kernel(order_ref, *refs):
        give_ref, keep_ref, held, left_ref, turned_ref, sems, left_sems = refs[2 * n :]
        come = [
            pltpu.make_async_copy(ref, left_ref.at[i], left_sems.at[i])
            for i, ref in enumerate(refs[:n])
        ]
        for copy in come:
            copy.start()
        for b in range(4):
            where = pl.ds(pl.multiple_of(order_ref[b] * cols, cols), cols)
            for i, right in enumerate(refs[n : 2 * n]):
                there = held.at[b, i * rows : (i + 1) * rows, :]
                pltpu.make_async_copy(right.at[:, where], there, sems.at[b, i]).start()
        for copy in come:
            copy.wait()
        turned_ref[...] = jnp.concatenate([left_ref[i] for i in range(n)], axis=0).T

        def column_part(b, _):
            for i, right in enumerate(refs[n : 2 * n]):
                there = held.at[b, i * rows : (i + 1) * rows, :]
                pltpu.make_async_copy(right.at[:, :cols], there, sems.at[b, i]).wait()
            part = jnp.dot(turned_ref[...], held[b], preferred_element_type=F32)

            @pl.when(b < 2)
            def _():
                give_ref[b] = part.astype(BF)

            @pl.when(b >= 2)
            def _():
                keep_ref[b - 2] = part

            return 0

        lax.fori_loop(0, 4, column_part, 0)

    return call(
        kernel,
        [jax.ShapeDtypeStruct((2, hid, cols), BF), jax.ShapeDtypeStruct((2, hid, cols), F32)],
        [SCALARS] + [ANYWHERE] * (2 * n),
        12 * hid * cols + 8 * n * rows * cols,
        flops=8 * n * rows * hid * cols,
        limit=BIG_LIMIT,
        scratch_shapes=[
            pltpu.VMEM((4, n * rows, cols), BF),
            pltpu.VMEM((n, rows, hid), BF),
            pltpu.VMEM((hid, n * rows), BF),
            pltpu.SemaphoreType.DMA((4, n)),
            pltpu.SemaphoreType.DMA((n,)),
        ],
    )(order, *lefts, *rights)


def per_device(tokens, out_grad, gate_weight, up_weight, down_weight, block_mask, assignment):
    own, width = tokens.shape
    hid, cols = gate_weight.shape
    panels, col_blocks = hid // BLK, cols // BLK
    unit = 2 * own
    x_hi, core, z = (lax.axis_index(a) for a in ("x_hi", "core", "z"))
    place = jnp.stack(
        [2 * x_hi + core, 2 * (1 - x_hi) + core, 2 * x_hi + 1 - core, 2 * (1 - x_hi) + 1 - core]
    )
    tie = lax.optimization_barrier

    panel_ids = lax.broadcasted_iota(jnp.int32, (panels, block_mask.shape[1]), 1)
    selector = (assignment[:, None] == panel_ids).astype(F32)
    slot_mask = jnp.einsum("sp,mpb->msb", selector, block_mask.astype(F32))
    slot_mask = lax.dynamic_slice_in_dim(slot_mask, place[0] * col_blocks, col_blocks, 2)
    keep = jnp.repeat(slot_mask, BLK, axis=2)

    mine = pack([tokens, out_grad])
    tok16, grd16 = by_array(mine, fetch(mine, "x_lo", 1))
    kept = mask_weights([gate_weight, up_weight, down_weight], keep.reshape(-1, cols))
    tok16, grd16, kept = tie((tok16, grd16, kept))

    t1, t3, t2 = fetch(tok16, "y", 1), fetch(tok16, "y", -1), fetch(tok16, "y", 2)
    z1, z7 = fetch(grd16, "z", 1), fetch(grd16, "z", -1)
    z1, z7, t1, t3, t2 = tie((z1, z7, t1, t3, t2))
    tok = unpack(
        [([2 * dy, 2 * dy + 1], [t]) for dy, t in enumerate((tok16, t1, t2, t3))], N_X * N_Y, own, width
    )
    tok = lax.all_gather(tok, "z", axis=0, tiled=True)
    away = [fetch(kept[0], "x_hi", 1)]
    beside_kept = [fetch(half, "core", 1) for half in kept]
    z2, z6, beside_kept = tie((fetch(z1, "z", 1), fetch(z7, "z", -1), beside_kept))
    near = stack([grd16, z1, z7, z2, z6])
    cut = near.shape[1] // 2
    n1, n3 = fetch(near, "y", 1), fetch(near, "y", -1)
    z3, z5 = tie((fetch(z2, "z", 1), fetch(z6, "z", -1)))
    z4 = [fetch(z3[:, :cut], "z", 1), fetch(z5[:, cut:], "z", -1)]
    z4, later = tie((z4, kept[1]))
    rest = join([[z3], [z5], z4])
    n1, n3, rest, away = tie((n1, n3, rest, away))
    n2 = [fetch(n1[:, :cut], "y", 1), fetch(n3[:, cut:], "y", -1)]
    r1, r3 = fetch(rest, "y", 1), fetch(rest, "y", -1)
    away = [away[0], fetch(later, "x_hi", 1)]
    kept_turned, beside_turned = turn(kept), turn(beside_kept)
    n2, r1, r3, away, kept_turned, beside_turned = tie(
        (n2, r1, r3, away, kept_turned, beside_turned)
    )
    r2 = [fetch(r1[:, :cut], "y", 1), fetch(r3[:, cut:], "y", -1)]
    beside_away = [fetch(half, "core", 1) for half in away]
    blocks = [kept, away, beside_kept, beside_away]
    turned = [kept_turned, turn(away), beside_turned, turn(beside_away)]
    tok, r2, turned = tie((tok, r2, turned))
    pieces = []
    for dy, n, r in ((0, [near], [rest]), (1, [n1], [r1]), (2, n2, r2), (3, [n3], [r3])):
        for offsets, held in (((0, 1, 7, 2, 6), n), ((3, 5, 4), r)):
            pieces.append(([2 * (N_Z * dy + dz) + dx for dz in offsets for dx in range(N_X)], held))
    by_z, grd, hidden, total = middle(z[None], place, tok, pieces, turned, blocks, own)
    total = lax.psum_scatter(total, "z", scatter_dimension=0, tiled=True)

    order = place[::-1]
    give_a, keep_a = weight_grads(order, [by_z], [tok])
    give_a = fetch(give_a, "core", 1)
    give_b, keep_b = weight_grads(order, [hidden], [grd])
    give_a, give_b, keep_b = tie((give_a, give_b, keep_b))
    far_a = fetch((keep_a[0] + give_a[0].astype(F32)).astype(BF), "x_hi", 1)
    give_b = fetch(give_b, "core", 1)
    far_b = fetch((keep_b[0] + give_b[0].astype(F32)).astype(BF), "x_hi", 1)

    def finish(keep_sum, give, far, rows):
        total = keep_sum[1] + give[1].astype(F32) + far.astype(F32)
        total = total.reshape(-1, panels, BLK, cols) * rows[:, :, None, :]
        return total.astype(BF).reshape(-1, hid, cols)

    gate_up_grad = finish(keep_a, give_a, far_a, keep[:2])
    down_grad = finish(keep_b, give_b, far_b, keep[2:])

    parts = deal(total, own)
    parts = [parts[0]] + [fetch(parts[dy], "y", -dy) for dy in (2, 1, 3)]

    def last(*parts):
        both = sum(part.astype(F32) for part in parts)
        return both[: own - 1], both[own - 1 :]

    parts, gate_up_grad, down_grad = tie((parts, gate_up_grad, down_grad))
    mine, other = local(last, *parts)
    input_grad = place_rows(place, mine, fetch(other, "x_lo", 1))
    return (input_grad, gate_up_grad[0], gate_up_grad[1], down_grad[0])


def solution(mesh):
    fine = Mesh(mesh.devices.reshape(SIZES), AXES)
    rows = P(DP + MP, None)
    weights = P(MP, DP)
    return jax.shard_map(
        per_device,
        mesh=fine,
        in_specs=(rows, rows, weights, weights, weights, P(), P(MP)),
        out_specs=(rows, weights, weights, weights),
        check_vma=False,
    )
```
